512 devices in a mesh: ctx: 64 (over y, z), head: 8 (over x, core).
Axes of the slice: x: 4, y: 8, z: 8, core: 2. Of those that a mesh axis runs over, the one named last changes fastest.
Arguments:
- queries: bfloat16 [32768, 6144], P(('ctx', 'head')), may hold values from -7 to 7
- keys: bfloat16 [32768, 1024], P(('ctx', 'head')), may hold values from -7 to 7
- values: bfloat16 [32768, 1024], P(('ctx', 'head')), may hold values from -6 to 6
- outputs: bfloat16 [32768, 6144], P(('ctx', 'head')), may hold values from -3 to 3
- grad_out: bfloat16 [32768, 6144], P(('ctx', 'head')), may hold values from -6 to 6
- first_block: int32 [128], replicated, may hold values from 0 to 126, as said below
Outputs:
- grad_queries: bfloat16 [32768, 6144], P(('ctx', 'head'))
- grad_keys: bfloat16 [32768, 1024], P(('ctx', 'head'))
- grad_values: bfloat16 [32768, 1024], P(('ctx', 'head'))
The draws below stay inside these ranges and needn't reach their ends.
Inputs may be any that keep to these rules, and one draw needn't show every extreme that they name: first_block[c] lies between max(0, c - 3) and c; for the last block it is 124, and for the block before it it is 126.
All inputs are finite; a program needn't handle non-finite values.
Results may differ from the reference program's by a relative error of at most 0.0085.
Values may be sent and summed in bfloat16 or wider, within the bound.
A program may use at most 128 MiB of HBM per device.

```python
import jax
import jax.numpy as jnp
from jax import lax

HEADS = 48
KV_HEADS = 8
HEAD_DIM = 128
BLOCK = 256
WINDOW = 4
GROUP = 6
BLOCK_COUNT = 128
TOKENS = 32768


def draw_queries(key, part):
    key = jax.random.fold_in(key, 1)
    base = jnp.clip(jax.random.normal(key, (TOKENS, HEADS * HEAD_DIM), jnp.float32), -6.0, 6.0)
    return base.astype(jnp.bfloat16)


def draw_keys(key, part):
    key = jax.random.fold_in(key, 2)
    base = jnp.clip(jax.random.normal(key, (TOKENS, KV_HEADS * HEAD_DIM), jnp.float32), -6.0, 6.0)
    return base.astype(jnp.bfloat16)


def draw_first_block(key, part):
    key = jax.random.fold_in(key, 3)
    indices = jnp.arange(BLOCK_COUNT, dtype=jnp.int32)
    spans = jax.random.randint(key, (BLOCK_COUNT,), 1, WINDOW + 1, dtype=jnp.int32)
    spans = jnp.where(indices == BLOCK_COUNT - 2, 1, spans)
    spans = jnp.where(indices == BLOCK_COUNT - 1, WINDOW, spans)
    return jnp.maximum(indices - spans + 1, 0).astype(jnp.int32)


def shard_levels(key, extent, cuts, smallest, high):
    def one(axis_at, parts):
        draws = jax.random.uniform(jax.random.fold_in(jax.random.fold_in(key, 6), axis_at), (parts,), jnp.float32, smallest / len(cuts), high / len(cuts))
        return jnp.repeat(jnp.exp(draws), extent[axis_at] // parts).reshape((-1,) + (1,) * (len(extent) - axis_at - 1))

    loudness = one(*cuts[0])
    for cut in cuts[1:]:
        loudness = loudness * one(*cut)
    return loudness


def centred(key, shape, width, most, pieces=(), kind=jnp.bfloat16):
    entries = width * jax.random.normal(key, shape, jnp.float32)
    if pieces:
        entries = entries * shard_levels(key, shape, pieces, -0.22, 0.18)
    return jnp.clip(entries, -most, most).astype(kind)


def setup_inputs(seed: int = 0) -> dict:
    key_list = jax.random.split(jax.random.key(seed), 7)
    queries = draw_queries(jax.random.fold_in(key_list[6], 71), 0)
    keys = draw_keys(jax.random.fold_in(key_list[6], 71), 0)
    values = centred(key_list[2], (TOKENS, KV_HEADS * HEAD_DIM), 1.0, 6.0, ((0, 512),))
    outputs = centred(key_list[3], (TOKENS, HEADS * HEAD_DIM), 0.5, 3.0, ((0, 512),))
    grad_out = centred(key_list[4], (TOKENS, HEADS * HEAD_DIM), 1.0, 6.0, ((0, 512),))
    first_block = draw_first_block(jax.random.fold_in(key_list[6], 71), 0)
    return dict(queries=queries, keys=keys, values=values, outputs=outputs, grad_out=grad_out, first_block=first_block)


def rounded(tensor):
    return lax.optimization_barrier(tensor.astype(jnp.bfloat16)).astype(jnp.float32)


def reference(queries, keys, values, outputs, grad_out, first_block):
    scaling = HEAD_DIM ** -0.5
    window_rows = WINDOW * BLOCK
    shaped = (TOKENS, HEADS, HEAD_DIM)
    correction = jnp.sum(grad_out.astype(jnp.float32).reshape(shaped) * outputs.astype(jnp.float32).reshape(shaped), axis=2)
    start_terms = jnp.zeros((TOKENS, KV_HEADS, HEAD_DIM), jnp.float32)

    def one_block(carry, block_index):
        key_grads, value_grads = carry
        first_query = block_index * BLOCK
        first_key_block = jnp.maximum(block_index - WINDOW + 1, 0).astype(jnp.int32)
        first_key = first_key_block * BLOCK
        query_part = lax.dynamic_slice_in_dim(queries, first_query, BLOCK, 0).astype(jnp.float32).reshape(BLOCK, KV_HEADS, GROUP, HEAD_DIM)
        grad_part = lax.dynamic_slice_in_dim(grad_out, first_query, BLOCK, 0).astype(jnp.float32).reshape(BLOCK, KV_HEADS, GROUP, HEAD_DIM)
        corr_part = lax.dynamic_slice_in_dim(correction, first_query, BLOCK, 0).reshape(BLOCK, KV_HEADS, GROUP).transpose(1, 2, 0)
        key_part = lax.dynamic_slice_in_dim(keys, first_key, window_rows, 0).astype(jnp.float32).reshape(window_rows, KV_HEADS, HEAD_DIM)
        value_part = lax.dynamic_slice_in_dim(values, first_key, window_rows, 0).astype(jnp.float32).reshape(window_rows, KV_HEADS, HEAD_DIM)
        key_blocks = first_key_block + jnp.arange(window_rows, dtype=jnp.int32) // BLOCK
        visible = (key_blocks >= first_block[block_index]) & (key_blocks <= block_index)
        mask = visible[None, None, None, :]
        scores = jnp.einsum("qcgd,kcd->cgqk", query_part, key_part) * scaling
        scores = jnp.where(mask, scores, -1e30)
        row_max = jnp.max(scores, axis=3, keepdims=True)
        weights = jnp.where(mask, jnp.exp(scores - row_max), 0.0)
        probs = weights / jnp.sum(weights, axis=3, keepdims=True)
        grad_probs = jnp.einsum("qcgd,kcd->cgqk", grad_part, value_part)
        grad_scores = rounded(probs * (grad_probs - corr_part[:, :, :, None]))
        probs_low = rounded(probs)
        grad_query = jnp.einsum("cgqk,kcd->qcgd", grad_scores, key_part) * scaling
        key_term = jnp.einsum("cgqk,qcgd->kcd", grad_scores, query_part) * scaling
        value_term = jnp.einsum("cgqk,qcgd->kcd", probs_low, grad_part)
        key_grads = lax.dynamic_update_slice_in_dim(key_grads, lax.dynamic_slice_in_dim(key_grads, first_key, window_rows, 0) + key_term, first_key, 0)
        value_grads = lax.dynamic_update_slice_in_dim(value_grads, lax.dynamic_slice_in_dim(value_grads, first_key, window_rows, 0) + value_term, first_key, 0)
        return (key_grads, value_grads), grad_query.reshape(BLOCK, HEADS * HEAD_DIM).astype(jnp.bfloat16)

    finals, query_grads = lax.scan(one_block, (start_terms, start_terms), jnp.arange(BLOCK_COUNT, dtype=jnp.int32))
    grad_queries = query_grads.reshape(TOKENS, HEADS * HEAD_DIM)
    grad_keys = finals[0].reshape(TOKENS, KV_HEADS * HEAD_DIM).astype(jnp.bfloat16)
    grad_values = finals[1].reshape(TOKENS, KV_HEADS * HEAD_DIM).astype(jnp.bfloat16)
    return (grad_queries, grad_keys, grad_values)
```

```python
import functools
import math

import jax
import jax.numpy as jnp
from jax import lax
from jax.experimental import pallas as pl
from jax.experimental.pallas import tpu as pltpu
from jax.sharding import PartitionSpec as P

HEAD_DIM = 128
BLOCK = 256
WINDOW = 4
MESH = pl.DeviceIdType.MESH
FAR = 1e30


def contract_last(a, b):
    return lax.dot_general(a, b, (((1,), (1,)), ((), ())), preferred_element_type=jnp.float32)


def kernel(
    parts,
    devices,
    group,
    q_hbm,
    k_hbm,
    v_hbm,
    o_hbm,
    g_hbm,
    first_ref,
    dq_hbm,
    dk_ref,
    dv_ref,
    q_own,
    g_own,
    o_own,
    corr_out,
    corr_in,
    corr_cols,
    qg,
    kv,
    k_turned,
    total,
    dq_out,
    terms,
    far_terms,
    arrived,
    load_sem,
    kv_sem,
    near_sem,
    far_sem,
    corr_sem,
    qg_sem,
    dq_sem,
    term_sem,
    far_term_sem,
    send_sem,
):
    rows = 2 * BLOCK // devices
    half = devices // 2
    width = group * HEAD_DIM
    span = 2 * BLOCK
    own = 3 * BLOCK
    scaling = HEAD_DIM ** (-0.5)
    to_exp2 = scaling * math.log2(math.e)
    p = lax.axis_index("ctx")
    h = lax.axis_index("head")

    def at(shift):
        return lax.rem(p + shift + parts, parts)

    def other(off):
        return lax.rem(h + off, devices)

    load_q = pltpu.make_async_copy(q_hbm, q_own, load_sem.at[0])
    load_g = pltpu.make_async_copy(g_hbm, g_own, load_sem.at[1])
    load_o = pltpu.make_async_copy(o_hbm, o_own, load_sem.at[2])
    load_q.start()
    load_g.start()
    load_o.start()

    barrier = pltpu.get_barrier_semaphore()

    def greet_row(off, carry):
        pl.semaphore_signal(barrier, inc=1, device_id=(p, other(off)), device_id_type=MESH)
        return carry

    def greet_near(off, carry):
        for shift in (1, -1):
            pl.semaphore_signal(
                barrier, inc=1, device_id=(at(shift), other(off)), device_id_type=MESH
            )
        return carry

    lax.fori_loop(1, devices, greet_row, 0)
    lax.fori_loop(0, devices, greet_near, 0)
    for shift in (2, -2):
        pl.semaphore_signal(barrier, inc=1, device_id=(at(shift), h), device_id_type=MESH)
    pl.semaphore_wait(barrier, 3 * devices + 1)

    def rows_at(start, count):
        return pl.ds(pl.multiple_of(start, 64), count)

    def lanes_at(start, count):
        return pl.ds(pl.multiple_of(start, HEAD_DIM), count)

    mine = rows_at(h * rows, rows)
    mine_kv = rows_at(own + h * rows, rows)

    for index, source in ((0, k_hbm), (1, v_hbm)):

        def send_kv(off, carry):
            d = other(off)
            pltpu.make_async_remote_copy(
                src_ref=source.at[:, lanes_at(d * HEAD_DIM, HEAD_DIM)],
                dst_ref=kv.at[index, mine_kv],
                send_sem=send_sem.at[0],
                recv_sem=kv_sem.at[index],
                device_id=(p, d),
                device_id_type=MESH,
            ).start()
            return carry

        lax.fori_loop(1, devices, send_kv, 0)
        pltpu.make_async_copy(
            source.at[:, lanes_at(h * HEAD_DIM, HEAD_DIM)], kv.at[index, mine_kv], kv_sem.at[index]
        ).start()

    def send_heads(i, count, sem):
        for index, source in ((0, q_own), (1, g_own)):

            def send_part(off, carry):
                d = other(off)
                pltpu.make_async_remote_copy(
                    src_ref=source.at[:, lanes_at(d * width + i * HEAD_DIM, count * HEAD_DIM)],
                    dst_ref=qg.at[index, mine, lanes_at(i * HEAD_DIM, count * HEAD_DIM)],
                    send_sem=send_sem.at[2],
                    recv_sem=qg_sem.at[sem],
                    device_id=(p, d),
                    device_id_type=MESH,
                ).start()
                return carry

            lax.fori_loop(1, devices, send_part, 0)
            pltpu.make_async_copy(
                source.at[:, lanes_at(h * width + i * HEAD_DIM, count * HEAD_DIM)],
                qg.at[index, mine, lanes_at(i * HEAD_DIM, count * HEAD_DIM)],
                qg_sem.at[sem],
            ).start()

    def wait_heads(i, count, sem):
        part = qg.at[:, :, i * HEAD_DIM : (i + count) * HEAD_DIM]
        pltpu.make_async_copy(part, part, qg_sem.at[sem]).wait()

    load_q.wait()
    load_g.wait()
    send_heads(0, 2, 0)


    load_o.wait()
    row_of = lax.broadcasted_iota(jnp.int32, (16, width), 0)
    col_of = lax.broadcasted_iota(jnp.int32, (16, width), 1)
    pick = jnp.where((row_of % 8) == col_of // HEAD_DIM, 1.0, 0.0).astype(jnp.bfloat16)
    upper = lax.broadcasted_iota(jnp.int32, (16, rows), 0) < 8
    corr_out[...] = jnp.zeros_like(corr_out)
    for d in range(devices):
        cols = slice(d * width, (d + 1) * width)
        product = g_own[:, cols].astype(jnp.float32) * o_own[:, cols].astype(jnp.float32)
        high = product.astype(jnp.bfloat16)
        low = (product - high.astype(jnp.float32)).astype(jnp.bfloat16)
        corr = contract_last(pick, high) + contract_last(pick, low)
        corr_high = corr.astype(jnp.bfloat16).astype(jnp.float32)
        corr_out[d, :, 0:rows] = jnp.where(upper, corr_high, corr - corr_high).astype(jnp.bfloat16)

    def send_corr(off, carry):
        d = other(off)
        pltpu.make_async_remote_copy(
            src_ref=corr_out.at[d],
            dst_ref=corr_in.at[h],
            send_sem=send_sem.at[1],
            recv_sem=corr_sem,
            device_id=(p, d),
            device_id_type=MESH,
        ).start()
        return carry

    lax.fori_loop(1, devices, send_corr, 0)
    pltpu.make_async_copy(corr_out.at[h], corr_in.at[h], corr_sem).start()
    total[...] = jnp.zeros_like(total)

    total[...] = jnp.zeros_like(total)

    near, far = [], []
    for index in range(2):
        held = kv.at[index, own : own + span]
        pltpu.make_async_copy(held, held, kv_sem.at[index]).wait()
        near.append(
            pltpu.make_async_remote_copy(
                src_ref=held,
                dst_ref=kv.at[index, BLOCK : BLOCK + span],
                send_sem=send_sem.at[3],
                recv_sem=near_sem.at[index],
                device_id=(at(1), h),
                device_id_type=MESH,
            )
        )
        near[index].start()
        far.append(
            pltpu.make_async_remote_copy(
                src_ref=kv.at[index, 2 * BLOCK : 3 * BLOCK],
                dst_ref=kv.at[index, 0:BLOCK],
                send_sem=send_sem.at[4],
                recv_sem=far_sem.at[index],
                device_id=(at(1), h),
                device_id_type=MESH,
            )
        )
    total[...] = jnp.zeros_like(total)
    send_heads(2, 2, 1)

    for index in range(2):
        near[index].wait_recv()
        far[index].start()
    send_heads(4, 1, 2)
    send_heads(5, 1, 3)

    pltpu.make_async_copy(corr_in, corr_in, corr_sem).wait()
    for d in range(devices):
        piece = corr_in[d].astype(jnp.float32)
        square = jnp.concatenate([piece, jnp.zeros((112, HEAD_DIM), jnp.float32)], axis=0).T
        corr_cols[d * rows : (d + 1) * rows] = square[0:rows].astype(jnp.bfloat16)

    def turn(block):
        part = slice(block * BLOCK, (block + 1) * BLOCK)
        k_turned[:, part] = kv[0, part].astype(jnp.float32).T.astype(jnp.bfloat16)

    turn(3)
    turn(4)
    turn(1)
    turn(2)

    def round_terms(start, count):
        for r in range(start, start + count):
            part = slice(r * rows, (r + 1) * rows)
            terms[r, 0] = (total[0, part] * scaling).astype(jnp.bfloat16)
            terms[r, 1] = total[1, part].astype(jnp.bfloat16)

    def term_copy(r, distance, d):
        return pltpu.make_async_remote_copy(
            src_ref=terms.at[r],
            dst_ref=arrived.at[distance, h],
            send_sem=send_sem.at[6],
            recv_sem=term_sem.at[distance],
            device_id=(at(-distance), d),
            device_id_type=MESH,
        )

    pass_back = pltpu.make_async_remote_copy(
        src_ref=terms.at[0:half],
        dst_ref=far_terms,
        send_sem=send_sem.at[7],
        recv_sem=far_term_sem,
        device_id=(at(-2), h),
        device_id_type=MESH,
    )

    def send_dq(i, count):
        cols = slice(i * HEAD_DIM, (i + count) * HEAD_DIM)
        target = dq_hbm.at[:, lanes_at(h * width + i * HEAD_DIM, count * HEAD_DIM)]

        def send_part(off, carry):
            d = other(off)
            pltpu.make_async_remote_copy(
                src_ref=dq_out.at[rows_at(d * rows, rows), cols],
                dst_ref=target,
                send_sem=send_sem.at[5],
                recv_sem=dq_sem,
                device_id=(p, d),
                device_id_type=MESH,
            ).start()
            return carry

        lax.fori_loop(1, devices, send_part, 0)
        pltpu.make_async_copy(dq_out.at[mine, cols], target, dq_sem).start()

    def send_half(i, count, late):
        cols = slice(i * HEAD_DIM, (i + count) * HEAD_DIM)
        target = dq_hbm.at[:, lanes_at(h * width + i * HEAD_DIM, count * HEAD_DIM)]

        def send_part(d, carry):
            source = dq_out.at[rows_at(d * rows, rows), cols]

            @pl.when(d != h)
            def _():
                pltpu.make_async_remote_copy(
                    src_ref=source,
                    dst_ref=target,
                    send_sem=send_sem.at[5],
                    recv_sem=dq_sem,
                    device_id=(p, d),
                    device_id_type=MESH,
                ).start()

            @pl.when(d == h)
            def _():
                pltpu.make_async_copy(source, target, dq_sem).start()

            return carry

        lax.fori_loop(late * half, (late + 1) * half, send_part, 0)

    reach = WINDOW * BLOCK
    lane = lax.broadcasted_iota(jnp.int32, (reach, HEAD_DIM), 1)

    def products(late, i):
        query_rows = rows_at(late * BLOCK, BLOCK)
        key_rows = rows_at(late * BLOCK, reach)
        head_cols = lanes_at(i * HEAD_DIM, HEAD_DIM)
        q = qg[0, query_rows, head_cols]
        g = qg[1, query_rows, head_cols]
        score = contract_last(kv[0, key_rows, :], q)
        g_wide = jnp.concatenate([g, corr_cols[query_rows, :]], axis=1)
        minus = jnp.where((lane == i) | (lane == i + 8), -1.0, 0.0).astype(jnp.bfloat16)
        v_wide = jnp.concatenate([kv[1, key_rows, :], minus], axis=1)
        return q, g, score, contract_last(v_wide, g_wide)

    def softmax(late, score):
        first = first_ref[2 * p + late]
        tiles = [score[t * BLOCK : (t + 1) * BLOCK] for t in range(WINDOW)]
        biases = [
            jnp.where(first <= 2 * p + late - 3 + t, 0.0, -FAR).astype(jnp.float32)
            for t in range(WINDOW)
        ]
        peak = None
        for t in range(WINDOW):
            top = jnp.max(tiles[t], axis=0, keepdims=True) + biases[t]
            peak = top if peak is None else jnp.maximum(peak, top)
        level = peak * to_exp2
        weights = [
            jnp.exp2(tiles[t] * to_exp2 - (level - biases[t])) for t in range(WINDOW)
        ]
        weights = jnp.concatenate(weights, axis=0)
        return weights * (1.0 / jnp.sum(weights, axis=0, keepdims=True))

    def returned(late, i, q, g, probs, grads):
        grad_scores = (probs * grads).astype(jnp.bfloat16)
        key_term = jnp.dot(grad_scores, q, preferred_element_type=jnp.float32)
        value_term = jnp.dot(probs.astype(jnp.bfloat16), g, preferred_element_type=jnp.float32)
        dq_turned = jnp.dot(
            k_turned[:, lanes_at(late * BLOCK, reach)],
            grad_scores,
            preferred_element_type=jnp.float32,
        )
        query_rows = rows_at(late * BLOCK, BLOCK)
        dq_out[query_rows, lanes_at(i * HEAD_DIM, HEAD_DIM)] = (
            (dq_turned * scaling).T.astype(jnp.bfloat16)
        )
        key_rows = rows_at(late * BLOCK, reach)
        total[0, key_rows, :] += key_term
        total[1, key_rows, :] += value_term

    def pair(k, carry):
        late = (5 - k) // 5 + k // 5
        late_b = k % 2 + (5 - k) // 5
        i = k - ((k + 1) // 2) % 2
        i_b = k + (k // 2 + 1) % 2 - k // 5

        @pl.when(k == 1)
        def _():
            far[0].wait_recv()
            far[1].wait_recv()
            turn(0)
            wait_heads(2, 2, 1)

        @pl.when(k == 4)
        def _():
            wait_heads(4, 1, 2)
            wait_heads(5, 1, 3)

        q, g, score, grads = products(late, i)
        q_b, g_b, score_b, grads_b = products(late_b, i_b)
        probs = softmax(late, score)
        probs_b = softmax(late_b, score_b)
        returned(late, i, q, g, probs, grads)
        returned(late_b, i_b, q_b, g_b, probs_b, grads_b)

        @pl.when(k == 2)
        def _():
            send_dq(0, 2)

        @pl.when(k == 3)
        def _():
            send_dq(2, 2)

        @pl.when(k == 4)
        def _():
            round_terms(0, half)
            pass_back.start()
            send_half(4, 2, 0)

        return carry

    wait_heads(0, 2, 0)
    lax.fori_loop(0, group, pair, 0)

    round_terms(half, devices)

    def send_near(off, carry):
        d = other(off)
        term_copy(half + d, 1, d).start()
        return carry

    lax.fori_loop(0, devices, send_near, 0)
    send_half(4, 2, 1)
    def send_own(d, carry):
        source = terms.at[half + devices + d]

        @pl.when(d != h)
        def _():
            term_copy(half + devices + d, 0, d).start()

        @pl.when(d == h)
        def _():
            pltpu.make_async_copy(source, arrived.at[0, h], term_sem.at[0]).start()

        return carry

    round_terms(half + devices, half)
    lax.fori_loop(0, half, send_own, 0)
    pass_back.wait_recv()
    for r in range(half):
        at_row = half + devices + half + r
        part = slice(at_row * rows, (at_row + 1) * rows)
        terms[at_row, 0] = (
            total[0, part] * scaling + far_terms[r, 0].astype(jnp.float32)
        ).astype(jnp.bfloat16)
        terms[at_row, 1] = (total[1, part] + far_terms[r, 1].astype(jnp.float32)).astype(
            jnp.bfloat16
        )
    lax.fori_loop(half, devices, send_own, 0)

    pltpu.make_async_copy(arrived.at[0], arrived.at[0], term_sem.at[0]).wait()
    pltpu.make_async_copy(arrived.at[1], arrived.at[1], term_sem.at[1]).wait()
    for d in range(devices):
        cols = slice(d * HEAD_DIM, (d + 1) * HEAD_DIM)
        for index, out in ((0, dk_ref), (1, dv_ref)):
            held = arrived[0, d, index].astype(jnp.float32)
            more = arrived[1, d, index].astype(jnp.float32)
            out[:, cols] = (held + more).astype(jnp.bfloat16)
    pltpu.make_async_copy(dq_hbm, dq_hbm, dq_sem).wait()

    most = span - rows

    def left(view, index):
        pltpu.make_async_copy(view, view, send_sem.at[index]).wait()

    left(kv.at[:, 0:most], 0)
    left(corr_in.at[0 : devices - 1], 1)
    left(qg.at[:, 0:most], 2)
    left(kv.at[:, 0:span], 3)
    left(kv.at[:, 0:BLOCK], 4)
    pass_back.wait_send()
    left(dq_out.at[0:most], 5)
    left(terms.at[0 : 2 * devices - 1], 6)


def solution(mesh):
    parts = mesh.shape["ctx"]
    devices = mesh.shape["head"]
    rows = 2 * BLOCK // devices

    def local(queries, keys, values, outputs, grad_out, first_block):
        group = queries.shape[1] // keys.shape[1]
        hbm = pl.BlockSpec(memory_space=pl.ANY)
        vmem = pl.BlockSpec(memory_space=pltpu.VMEM)
        low, full = jnp.bfloat16, jnp.float32
        dma = pltpu.SemaphoreType.DMA
        width = queries.shape[1] // devices
        band = 5 * BLOCK
        return pl.pallas_call(
            functools.partial(kernel, parts, devices, group),
            out_shape=(
                jax.ShapeDtypeStruct(queries.shape, low),
                jax.ShapeDtypeStruct(keys.shape, low),
                jax.ShapeDtypeStruct(values.shape, low),
            ),
            in_specs=[hbm] * 5 + [pl.BlockSpec(memory_space=pltpu.SMEM)],
            out_specs=(hbm, vmem, vmem),
            scratch_shapes=[
                pltpu.VMEM(queries.shape, low),
                pltpu.VMEM(grad_out.shape, low),
                pltpu.VMEM(outputs.shape, low),
                pltpu.VMEM((devices, 16, HEAD_DIM), low),
                pltpu.VMEM((devices, 16, HEAD_DIM), low),
                pltpu.VMEM((2 * BLOCK, HEAD_DIM), low),
                pltpu.VMEM((2, 2 * BLOCK, width), low),
                pltpu.VMEM((2, band, HEAD_DIM), low),
                pltpu.VMEM((HEAD_DIM, band), low),
                pltpu.VMEM((2, band, HEAD_DIM), full),
                pltpu.VMEM((2 * BLOCK, width), low),
                pltpu.VMEM((band // rows, 2, rows, HEAD_DIM), low),
                pltpu.VMEM((devices // 2, 2, rows, HEAD_DIM), low),
                pltpu.VMEM((2, devices, 2, rows, HEAD_DIM), low),
                dma((3,)),
                dma((2,)),
                dma((2,)),
                dma((2,)),
                dma,
                dma((4,)),
                dma,
                dma((2,)),
                dma,
                dma((8,)),
            ],
            compiler_params=pltpu.CompilerParams(
                collective_id=0,
                has_side_effects=True,
                vmem_limit_bytes=63 * 1024 * 1024,
            ),
            cost_estimate=pl.CostEstimate(
                flops=48 * 5 * 2 * 256 * 256 * 128, bytes_accessed=8_000_000, transcendentals=0
            ),
        )(queries, keys, values, outputs, grad_out, first_block)

    placed = P(("ctx", "head"), None)
    return jax.shard_map(
        local,
        mesh=mesh,
        in_specs=(placed,) * 5 + (P(),),
        out_specs=(placed,) * 3,
        check_vma=False,
    )
```

```python
import functools
import math

import jax
import jax.numpy as jnp
from jax import lax
from jax.experimental import pallas as pl
from jax.experimental.pallas import tpu as pltpu
from jax.sharding import PartitionSpec as P

HEAD_DIM = 128
BLOCK = 256
WINDOW = 4
MESH = pl.DeviceIdType.MESH
FAR = 1e30


def contract_last(a, b):
    return lax.dot_general(a, b, (((1,), (1,)), ((), ())), preferred_element_type=jnp.float32)


def kernel(
    parts,
    devices,
    group,
    q_hbm,
    k_hbm,
    v_hbm,
    o_hbm,
    g_hbm,
    first_ref,
    dq_hbm,
    dkv_ref,
    q_own,
    g_own,
    o_own,
    corr_out,
    corr_in,
    corr_cols,
    qg,
    k_band,
    v_band,
    k_turned,
    total,
    dq_out,
    terms,
    far_terms,
    arrived,
    load_sem,
    kv_sem,
    near_sem,
    far_sem,
    corr_sem,
    qg_sem,
    dq_sem,
    term_sem,
    far_term_sem,
    send_sem,
):
    rows = 2 * BLOCK // devices
    half = devices // 2
    width = group * HEAD_DIM
    span = 2 * BLOCK
    own = 3 * BLOCK
    scaling = HEAD_DIM ** (-0.5)
    to_exp2 = scaling * math.log2(math.e)
    p = lax.axis_index("ctx")
    h = lax.axis_index("head")

    def at(shift):
        return lax.rem(p + shift + parts, parts)

    def other(off):
        return lax.rem(h + off, devices)

    load_q = pltpu.make_async_copy(q_hbm, q_own, load_sem.at[0])
    load_g = pltpu.make_async_copy(g_hbm, g_own, load_sem.at[1])
    load_o = pltpu.make_async_copy(o_hbm, o_own, load_sem.at[2])
    load_q.start()
    load_g.start()
    load_o.start()

    barrier = pltpu.get_barrier_semaphore()

    def greet_row(off, carry):
        pl.semaphore_signal(barrier, inc=1, device_id=(p, other(off)), device_id_type=MESH)
        return carry

    def greet_near(off, carry):
        for shift in (1, -1):
            pl.semaphore_signal(
                barrier, inc=1, device_id=(at(shift), other(off)), device_id_type=MESH
            )
        return carry

    lax.fori_loop(1, devices, greet_row, 0)
    lax.fori_loop(0, devices, greet_near, 0)
    for shift in (2, -2):
        pl.semaphore_signal(barrier, inc=1, device_id=(at(shift), h), device_id_type=MESH)
    pl.semaphore_wait(barrier, 3 * devices + 1)

    def rows_at(start, count):
        return pl.ds(pl.multiple_of(start, 64), count)

    def lanes_at(start, count):
        return pl.ds(pl.multiple_of(start, HEAD_DIM), count)

    mine = rows_at(h * rows, rows)
    mine_kv = rows_at(own + h * rows, rows)

    for index, source, band in ((0, k_hbm, k_band), (1, v_hbm, v_band)):

        def send_kv(off, carry):
            d = other(off)
            pltpu.make_async_remote_copy(
                src_ref=source.at[:, lanes_at(d * HEAD_DIM, HEAD_DIM)],
                dst_ref=band.at[mine_kv, 0:HEAD_DIM],
                send_sem=send_sem.at[0],
                recv_sem=kv_sem.at[index],
                device_id=(p, d),
                device_id_type=MESH,
            ).start()
            return carry

        lax.fori_loop(1, devices, send_kv, 0)
        pltpu.make_async_copy(
            source.at[:, lanes_at(h * HEAD_DIM, HEAD_DIM)], band.at[mine_kv, 0:HEAD_DIM], kv_sem.at[index]
        ).start()

    def send_heads(i, count, sem):
        for index, source in ((0, q_own), (1, g_own)):

            def send_part(off, carry):
                d = other(off)
                pltpu.make_async_remote_copy(
                    src_ref=source.at[:, lanes_at(d * width + i * HEAD_DIM, count * HEAD_DIM)],
                    dst_ref=qg.at[index, mine, lanes_at(i * HEAD_DIM, count * HEAD_DIM)],
                    send_sem=send_sem.at[2],
                    recv_sem=qg_sem.at[sem],
                    device_id=(p, d),
                    device_id_type=MESH,
                ).start()
                return carry

            lax.fori_loop(1, devices, send_part, 0)
            pltpu.make_async_copy(
                source.at[:, lanes_at(h * width + i * HEAD_DIM, count * HEAD_DIM)],
                qg.at[index, mine, lanes_at(i * HEAD_DIM, count * HEAD_DIM)],
                qg_sem.at[sem],
            ).start()

    def wait_heads(i, count, sem):
        part = qg.at[:, :, i * HEAD_DIM : (i + count) * HEAD_DIM]
        pltpu.make_async_copy(part, part, qg_sem.at[sem]).wait()

    load_q.wait()
    load_g.wait()
    send_heads(0, 2, 0)


    load_o.wait()
    row_of = lax.broadcasted_iota(jnp.int32, (16, width), 0)
    col_of = lax.broadcasted_iota(jnp.int32, (16, width), 1)
    pick = jnp.where((row_of % 8) == col_of // HEAD_DIM, 1.0, 0.0).astype(jnp.bfloat16)
    upper = lax.broadcasted_iota(jnp.int32, (16, rows), 0) < 8
    corr_out[...] = jnp.zeros_like(corr_out)
    for d in range(devices):
        cols = slice(d * width, (d + 1) * width)
        product = g_own[:, cols].astype(jnp.float32) * o_own[:, cols].astype(jnp.float32)
        high = product.astype(jnp.bfloat16)
        low = (product - high.astype(jnp.float32)).astype(jnp.bfloat16)
        corr = contract_last(pick, high) + contract_last(pick, low)
        corr_high = corr.astype(jnp.bfloat16).astype(jnp.float32)
        corr_out[d, :, 0:rows] = jnp.where(upper, corr_high, corr - corr_high).astype(jnp.bfloat16)

    def send_corr(off, carry):
        d = other(off)
        pltpu.make_async_remote_copy(
            src_ref=corr_out.at[d],
            dst_ref=corr_in.at[h],
            send_sem=send_sem.at[1],
            recv_sem=corr_sem,
            device_id=(p, d),
            device_id_type=MESH,
        ).start()
        return carry

    lax.fori_loop(1, devices, send_corr, 0)
    pltpu.make_async_copy(corr_out.at[h], corr_in.at[h], corr_sem).start()
    total[...] = jnp.zeros_like(total)
    v_band[:, HEAD_DIM:] = jnp.full((5 * BLOCK, HEAD_DIM), -1.0, jnp.bfloat16)


    near, far = [], []
    for index, band in ((0, k_band), (1, v_band)):
        held = band.at[own : own + span, 0:HEAD_DIM]
        pltpu.make_async_copy(held, held, kv_sem.at[index]).wait()
        near.append(
            pltpu.make_async_remote_copy(
                src_ref=held,
                dst_ref=band.at[BLOCK : BLOCK + span, 0:HEAD_DIM],
                send_sem=send_sem.at[3],
                recv_sem=near_sem.at[index],
                device_id=(at(1), h),
                device_id_type=MESH,
            )
        )
        near[index].start()
        far.append(
            pltpu.make_async_remote_copy(
                src_ref=band.at[2 * BLOCK : 3 * BLOCK, 0:HEAD_DIM],
                dst_ref=band.at[0:BLOCK, 0:HEAD_DIM],
                send_sem=send_sem.at[4],
                recv_sem=far_sem.at[index],
                device_id=(at(1), h),
                device_id_type=MESH,
            )
        )
    send_heads(2, 2, 1)

    def turn(block):
        part = slice(block * BLOCK, (block + 1) * BLOCK)
        k_turned[:, part] = k_band[part].astype(jnp.float32).T.astype(jnp.bfloat16)

    turn(3)
    turn(4)
    near[0].wait_recv()
    far[0].start()
    turn(1)
    turn(2)

    pltpu.make_async_copy(corr_in, corr_in, corr_sem).wait()
    for d in range(devices):
        piece = corr_in[d].astype(jnp.float32)
        square = jnp.concatenate([piece, jnp.zeros((112, HEAD_DIM), jnp.float32)], axis=0).T
        corr_cols[d * rows : (d + 1) * rows] = square[0:rows].astype(jnp.bfloat16)

    near[1].wait_recv()
    far[1].start()
    send_heads(4, 2, 2)


    def round_terms(start, count):
        for r in range(start, start + count):
            part = slice(r * rows, (r + 1) * rows)
            terms[r, 0] = (total[0, part] * scaling).astype(jnp.bfloat16)
            terms[r, 1] = total[1, part].astype(jnp.bfloat16)

    def term_copy(r, distance, d):
        return pltpu.make_async_remote_copy(
            src_ref=terms.at[r],
            dst_ref=arrived.at[distance, h],
            send_sem=send_sem.at[6],
            recv_sem=term_sem.at[distance],
            device_id=(at(-distance), d),
            device_id_type=MESH,
        )

    pass_back = pltpu.make_async_remote_copy(
        src_ref=terms.at[0:half],
        dst_ref=far_terms,
        send_sem=send_sem.at[7],
        recv_sem=far_term_sem,
        device_id=(at(-2), h),
        device_id_type=MESH,
    )

    def send_dq(i, count):
        cols = slice(i * HEAD_DIM, (i + count) * HEAD_DIM)
        target = dq_hbm.at[:, lanes_at(h * width + i * HEAD_DIM, count * HEAD_DIM)]

        def send_part(off, carry):
            d = other(off)
            pltpu.make_async_remote_copy(
                src_ref=dq_out.at[rows_at(d * rows, rows), cols],
                dst_ref=target,
                send_sem=send_sem.at[5],
                recv_sem=dq_sem,
                device_id=(p, d),
                device_id_type=MESH,
            ).start()
            return carry

        lax.fori_loop(1, devices, send_part, 0)
        pltpu.make_async_copy(dq_out.at[mine, cols], target, dq_sem).start()

    def send_half(i, count, late):
        cols = slice(i * HEAD_DIM, (i + count) * HEAD_DIM)
        target = dq_hbm.at[:, lanes_at(h * width + i * HEAD_DIM, count * HEAD_DIM)]

        def send_part(d, carry):
            source = dq_out.at[rows_at(d * rows, rows), cols]

            @pl.when(d != h)
            def _():
                pltpu.make_async_remote_copy(
                    src_ref=source,
                    dst_ref=target,
                    send_sem=send_sem.at[5],
                    recv_sem=dq_sem,
                    device_id=(p, d),
                    device_id_type=MESH,
                ).start()

            @pl.when(d == h)
            def _():
                pltpu.make_async_copy(source, target, dq_sem).start()

            return carry

        lax.fori_loop(late * half, (late + 1) * half, send_part, 0)

    reach = WINDOW * BLOCK
    lane = lax.broadcasted_iota(jnp.int32, (BLOCK, HEAD_DIM), 1)

    def pair(k, carry):
        late = ((k + 1) % 2) * (1 - k // 4) + (k // 4) * (k % 2)
        i = 2 * (k // 2)

        @pl.when(k == 1)
        def _():
            far[0].wait_recv()
            far[1].wait_recv()
            turn(0)

        @pl.when(k == 2)
        def _():
            wait_heads(2, 2, 1)

        @pl.when(k == 4)
        def _():
            wait_heads(4, 2, 2)

        query_rows = rows_at(late * BLOCK, BLOCK)
        key_rows = rows_at(late * BLOCK, reach)
        heads = [lanes_at((i + n) * HEAD_DIM, HEAD_DIM) for n in range(2)]
        q = jnp.concatenate([qg[0, query_rows, cols] for cols in heads], axis=0)
        g = jnp.concatenate([qg[1, query_rows, cols] for cols in heads], axis=0)
        corr = corr_cols[query_rows, :].astype(jnp.float32)
        corr = jnp.concatenate(
            [
                jnp.where((lane == i + n) | (lane == i + n + 8), corr, 0.0).astype(jnp.bfloat16)
                for n in range(2)
            ],
            axis=0,
        )
        score = contract_last(k_band[key_rows, :], q)
        grads = contract_last(v_band[key_rows, :], jnp.concatenate([g, corr], axis=1))
        first = first_ref[2 * p + late]
        tiles = [score[t * BLOCK : (t + 1) * BLOCK] for t in range(WINDOW)]
        biases = [
            jnp.where(first <= 2 * p + late - 3 + t, 0.0, -FAR).astype(jnp.float32)
            for t in range(WINDOW)
        ]
        peak = None
        for t in range(WINDOW):
            top = jnp.max(tiles[t], axis=0, keepdims=True) + biases[t]
            peak = top if peak is None else jnp.maximum(peak, top)
        level = peak * to_exp2
        weights = [
            jnp.exp2(tiles[t] * to_exp2 - (level - biases[t])) for t in range(WINDOW)
        ]
        weights = jnp.concatenate(weights, axis=0)
        probs = weights * (1.0 / jnp.sum(weights, axis=0, keepdims=True))
        grad_scores = (probs * grads).astype(jnp.bfloat16)
        total[0, key_rows, :] += jnp.dot(grad_scores, q, preferred_element_type=jnp.float32)
        total[1, key_rows, :] += jnp.dot(
            probs.astype(jnp.bfloat16), g, preferred_element_type=jnp.float32
        )
        dq_turned = jnp.dot(
            k_turned[:, lanes_at(late * BLOCK, reach)],
            grad_scores,
            preferred_element_type=jnp.float32,
        )
        dq = (dq_turned * scaling).T.astype(jnp.bfloat16)
        for n in range(2):
            dq_out[query_rows, heads[n]] = dq[n * BLOCK : (n + 1) * BLOCK]

        @pl.when(k == 1)
        def _():
            send_dq(0, 2)

        @pl.when(k == 3)
        def _():
            send_dq(2, 2)

        @pl.when(k == 4)
        def _():
            round_terms(0, half)
            pass_back.start()
            send_half(4, 2, 0)

        return carry

    wait_heads(0, 2, 0)
    lax.fori_loop(0, group, pair, 0)

    round_terms(half, devices)

    def send_near(off, carry):
        d = other(off)
        term_copy(half + d, 1, d).start()
        return carry

    lax.fori_loop(0, devices, send_near, 0)
    send_half(4, 2, 1)
    def send_own(d, carry):
        source = terms.at[half + devices + d]

        @pl.when(d != h)
        def _():
            term_copy(half + devices + d, 0, d).start()

        @pl.when(d == h)
        def _():
            pltpu.make_async_copy(source, arrived.at[0, h], term_sem.at[0]).start()

        return carry

    round_terms(half + devices, half)
    lax.fori_loop(0, half, send_own, 0)
    pass_back.wait_recv()
    for r in range(half):
        at_row = half + devices + half + r
        part = slice(at_row * rows, (at_row + 1) * rows)
        terms[at_row, 0] = (
            total[0, part] * scaling + far_terms[r, 0].astype(jnp.float32)
        ).astype(jnp.bfloat16)
        terms[at_row, 1] = (total[1, part] + far_terms[r, 1].astype(jnp.float32)).astype(
            jnp.bfloat16
        )
    lax.fori_loop(half, devices, send_own, 0)

    pltpu.make_async_copy(arrived.at[0], arrived.at[0], term_sem.at[0]).wait()
    pltpu.make_async_copy(arrived.at[1], arrived.at[1], term_sem.at[1]).wait()
    for d in range(devices):
        cols = slice(d * HEAD_DIM, (d + 1) * HEAD_DIM)
        for index in range(2):
            held = arrived[0, d, index].astype(jnp.float32)
            more = arrived[1, d, index].astype(jnp.float32)
            dkv_ref[index, :, cols] = (held + more).astype(jnp.bfloat16)
    pltpu.make_async_copy(dq_hbm, dq_hbm, dq_sem).wait()

    most = span - rows

    def left(view, index):
        pltpu.make_async_copy(view, view, send_sem.at[index]).wait()

    left(k_band.at[0 : 2 * most], 0)
    left(corr_in.at[0 : devices - 1], 1)
    left(qg.at[:, 0:most], 2)
    left(k_band.at[0 : 2 * span], 3)
    left(k_band.at[0 : 2 * BLOCK], 4)
    pass_back.wait_send()
    left(dq_out.at[0:most], 5)
    left(terms.at[0 : 2 * devices - 1], 6)


def finish(pieces, dq, dkv, dq_hbm, dk_hbm, dv_hbm, held, held_kv, in_sem, out_sem):
    rows = held.shape[0] // pieces
    legs = []
    for n in range(pieces):
        part = slice(n * rows, (n + 1) * rows)
        legs.append((dq.at[part], held.at[part], dq_hbm.at[part]))
    legs.append((dkv.at[0], held_kv.at[0], dk_hbm))
    legs.append((dkv.at[1], held_kv.at[1], dv_hbm))
    loads, stores = [], []
    for n, (source, between, target) in enumerate(legs):
        loads.append(pltpu.make_async_copy(source, between, in_sem.at[n]))
        stores.append(pltpu.make_async_copy(between, target, out_sem.at[n]))
        loads[n].start()
    for n in range(len(legs)):
        loads[n].wait()
        stores[n].start()
    for n in range(len(legs)):
        stores[n].wait()


def solution(mesh):
    parts = mesh.shape["ctx"]
    devices = mesh.shape["head"]
    rows = 2 * BLOCK // devices

    def local(queries, keys, values, outputs, grad_out, first_block):
        group = queries.shape[1] // keys.shape[1]
        hbm = pl.BlockSpec(memory_space=pl.ANY)
        vmem = pl.BlockSpec(memory_space=pltpu.VMEM)
        low, full = jnp.bfloat16, jnp.float32
        dma = pltpu.SemaphoreType.DMA
        width = queries.shape[1] // devices
        pieces = 4
        band = 5 * BLOCK
        dq, dkv = pl.pallas_call(
            functools.partial(kernel, parts, devices, group),
            out_shape=(
                jax.ShapeDtypeStruct(queries.shape, low),
                jax.ShapeDtypeStruct((2, *keys.shape), low),
            ),
            in_specs=[hbm] * 5 + [pl.BlockSpec(memory_space=pltpu.SMEM)],
            out_specs=(hbm, vmem),
            scratch_shapes=[
                pltpu.VMEM(queries.shape, low),
                pltpu.VMEM(grad_out.shape, low),
                pltpu.VMEM(outputs.shape, low),
                pltpu.VMEM((devices, 16, HEAD_DIM), low),
                pltpu.VMEM((devices, 16, HEAD_DIM), low),
                pltpu.VMEM((2 * BLOCK, HEAD_DIM), low),
                pltpu.VMEM((2, 2 * BLOCK, width), low),
                pltpu.VMEM((band, HEAD_DIM), low),
                pltpu.VMEM((band, 2 * HEAD_DIM), low),
                pltpu.VMEM((HEAD_DIM, band), low),
                pltpu.VMEM((2, band, HEAD_DIM), full),
                pltpu.VMEM((2 * BLOCK, width), low),
                pltpu.VMEM((band // rows, 2, rows, HEAD_DIM), low),
                pltpu.VMEM((devices // 2, 2, rows, HEAD_DIM), low),
                pltpu.VMEM((2, devices, 2, rows, HEAD_DIM), low),
                dma((3,)),
                dma((2,)),
                dma((2,)),
                dma((2,)),
                dma,
                dma((3,)),
                dma,
                dma((2,)),
                dma,
                dma((8,)),
            ],
            compiler_params=pltpu.CompilerParams(
                collective_id=0,
                has_side_effects=True,
                vmem_limit_bytes=63 * 1024 * 1024,
            ),
            cost_estimate=pl.CostEstimate(
                flops=48 * 5 * 2 * 256 * 256 * 128, bytes_accessed=8_000_000, transcendentals=0
            ),
        )(queries, keys, values, outputs, grad_out, first_block)
        return pl.pallas_call(
            functools.partial(finish, pieces),
            out_shape=(
                jax.ShapeDtypeStruct(queries.shape, low),
                jax.ShapeDtypeStruct(keys.shape, low),
                jax.ShapeDtypeStruct(values.shape, low),
            ),
            in_specs=[hbm] * 2,
            out_specs=(hbm,) * 3,
            scratch_shapes=[
                pltpu.VMEM(queries.shape, low),
                pltpu.VMEM((2, *keys.shape), low),
                dma((pieces + 2,)),
                dma((pieces + 2,)),
            ],
            compiler_params=pltpu.CompilerParams(vmem_limit_bytes=63 * 1024 * 1024),
        )(dq, dkv)

    placed = P(("ctx", "head"), None)
    return jax.shard_map(
        local,
        mesh=mesh,
        in_specs=(placed,) * 5 + (P(),),
        out_specs=(placed,) * 3,
        check_vma=False,
    )
```

```python
import functools
import math

import jax
import jax.numpy as jnp
from jax import lax
from jax.experimental import pallas as pl
from jax.experimental.pallas import tpu as pltpu
from jax.sharding import PartitionSpec as P

HEAD_DIM = 128
BLOCK = 256
WINDOW = 4
MESH = pl.DeviceIdType.MESH
FAR = 1e30


def contract_last(a, b):
    return lax.dot_general(a, b, (((1,), (1,)), ((), ())), preferred_element_type=jnp.float32)


def kernel(
    parts,
    devices,
    group,
    q_hbm,
    k_hbm,
    v_hbm,
    o_hbm,
    g_hbm,
    first_ref,
    dq_hbm,
    dkv_ref,
    q_own,
    g_own,
    o_own,
    corr_out,
    corr_in,
    corr_cols,
    qg,
    k_band,
    v_band,
    k_turned,
    scores_a,
    scores_b,
    grads_a,
    grads_b,
    total,
    dq_out,
    terms,
    far_terms,
    arrived,
    load_sem,
    kv_sem,
    near_sem,
    far_sem,
    corr_sem,
    qg_sem,
    dq_sem,
    term_sem,
    far_term_sem,
    send_sem,
):
    rows = 2 * BLOCK // devices
    half = devices // 2
    width = group * HEAD_DIM
    span = 2 * BLOCK
    own = 3 * BLOCK
    scaling = HEAD_DIM ** (-0.5)
    to_exp2 = scaling * math.log2(math.e)
    p = lax.axis_index("ctx")
    h = lax.axis_index("head")

    def at(shift):
        return lax.rem(p + shift + parts, parts)

    def other(off):
        return lax.rem(h + off, devices)

    barrier = pltpu.get_barrier_semaphore()

    def greet_row(off, carry):
        pl.semaphore_signal(barrier, inc=1, device_id=(p, other(off)), device_id_type=MESH)
        return carry

    def greet_near(off, carry):
        for shift in (1, -1):
            pl.semaphore_signal(
                barrier, inc=1, device_id=(at(shift), other(off)), device_id_type=MESH
            )
        return carry

    lax.fori_loop(1, devices, greet_row, 0)
    lax.fori_loop(0, devices, greet_near, 0)
    for shift in (2, -2):
        pl.semaphore_signal(barrier, inc=1, device_id=(at(shift), h), device_id_type=MESH)
    load_q = pltpu.make_async_copy(q_hbm, q_own, load_sem.at[0])
    load_g = pltpu.make_async_copy(g_hbm, g_own, load_sem.at[1])
    load_o = pltpu.make_async_copy(o_hbm, o_own, load_sem.at[2])
    load_q.start()
    load_g.start()
    load_o.start()

    pl.semaphore_wait(barrier, 3 * devices + 1)

    def rows_at(start, count):
        return pl.ds(pl.multiple_of(start, 64), count)

    def lanes_at(start, count):
        return pl.ds(pl.multiple_of(start, HEAD_DIM), count)

    mine = rows_at(h * rows, rows)
    mine_kv = rows_at(own + h * rows, rows)

    for index, source, band in ((0, k_hbm, k_band), (1, v_hbm, v_band)):

        def send_kv(off, carry):
            d = other(off)
            pltpu.make_async_remote_copy(
                src_ref=source.at[:, lanes_at(d * HEAD_DIM, HEAD_DIM)],
                dst_ref=band.at[mine_kv, 0:HEAD_DIM],
                send_sem=send_sem.at[0],
                recv_sem=kv_sem.at[index],
                device_id=(p, d),
                device_id_type=MESH,
            ).start()
            return carry

        lax.fori_loop(1, devices, send_kv, 0)
        pltpu.make_async_copy(
            source.at[:, lanes_at(h * HEAD_DIM, HEAD_DIM)], band.at[mine_kv, 0:HEAD_DIM], kv_sem.at[index]
        ).start()

    def send_heads(i, count, sem):
        for index, source in ((0, q_own), (1, g_own)):

            def send_part(off, carry):
                d = other(off)
                pltpu.make_async_remote_copy(
                    src_ref=source.at[:, lanes_at(d * width + i * HEAD_DIM, count * HEAD_DIM)],
                    dst_ref=qg.at[index, mine, lanes_at(i * HEAD_DIM, count * HEAD_DIM)],
                    send_sem=send_sem.at[2],
                    recv_sem=qg_sem.at[sem],
                    device_id=(p, d),
                    device_id_type=MESH,
                ).start()
                return carry

            lax.fori_loop(1, devices, send_part, 0)
            pltpu.make_async_copy(
                source.at[:, lanes_at(h * width + i * HEAD_DIM, count * HEAD_DIM)],
                qg.at[index, mine, lanes_at(i * HEAD_DIM, count * HEAD_DIM)],
                qg_sem.at[sem],
            ).start()

    def wait_heads(i, count, sem):
        part = qg.at[:, :, i * HEAD_DIM : (i + count) * HEAD_DIM]
        pltpu.make_async_copy(part, part, qg_sem.at[sem]).wait()

    load_q.wait()
    load_g.wait()
    send_heads(0, 2, 0)


    load_o.wait()
    row_of = lax.broadcasted_iota(jnp.int32, (16, width), 0)
    col_of = lax.broadcasted_iota(jnp.int32, (16, width), 1)
    pick = jnp.where((row_of % 8) == col_of // HEAD_DIM, 1.0, 0.0).astype(jnp.bfloat16)
    upper = lax.broadcasted_iota(jnp.int32, (16, rows), 0) < 8
    corr_out[...] = jnp.zeros_like(corr_out)
    for d in range(devices):
        cols = slice(d * width, (d + 1) * width)
        product = g_own[:, cols].astype(jnp.float32) * o_own[:, cols].astype(jnp.float32)
        high = product.astype(jnp.bfloat16)
        low = (product - high.astype(jnp.float32)).astype(jnp.bfloat16)
        corr = contract_last(pick, high) + contract_last(pick, low)
        corr_high = corr.astype(jnp.bfloat16).astype(jnp.float32)
        corr_out[d, :, 0:rows] = jnp.where(upper, corr_high, corr - corr_high).astype(jnp.bfloat16)

    def send_corr(off, carry):
        d = other(off)
        pltpu.make_async_remote_copy(
            src_ref=corr_out.at[d],
            dst_ref=corr_in.at[h],
            send_sem=send_sem.at[1],
            recv_sem=corr_sem,
            device_id=(p, d),
            device_id_type=MESH,
        ).start()
        return carry

    lax.fori_loop(1, devices, send_corr, 0)
    pltpu.make_async_copy(corr_out.at[h], corr_in.at[h], corr_sem).start()
    total[...] = jnp.zeros_like(total)
    v_band[:, HEAD_DIM:] = jnp.full((5 * BLOCK, HEAD_DIM), -1.0, jnp.bfloat16)


    near, far = [], []
    for index, band in ((0, k_band), (1, v_band)):
        held = band.at[own : own + span, 0:HEAD_DIM]
        pltpu.make_async_copy(held, held, kv_sem.at[index]).wait()
        near.append(
            pltpu.make_async_remote_copy(
                src_ref=held,
                dst_ref=band.at[BLOCK : BLOCK + span, 0:HEAD_DIM],
                send_sem=send_sem.at[3],
                recv_sem=near_sem.at[index],
                device_id=(at(1), h),
                device_id_type=MESH,
            )
        )
        near[index].start()
        far.append(
            pltpu.make_async_remote_copy(
                src_ref=band.at[2 * BLOCK : 3 * BLOCK, 0:HEAD_DIM],
                dst_ref=band.at[0:BLOCK, 0:HEAD_DIM],
                send_sem=send_sem.at[4],
                recv_sem=far_sem.at[index],
                device_id=(at(1), h),
                device_id_type=MESH,
            )
        )
    send_heads(2, 2, 1)

    def turn(block):
        part = slice(block * BLOCK, (block + 1) * BLOCK)
        k_turned[:, part] = k_band[part].astype(jnp.float32).T.astype(jnp.bfloat16)

    turn(3)
    turn(4)
    near[0].wait_recv()
    far[0].start()
    turn(1)
    turn(2)

    pltpu.make_async_copy(corr_in, corr_in, corr_sem).wait()
    for d in range(devices):
        piece = corr_in[d].astype(jnp.float32)
        square = jnp.concatenate([piece, jnp.zeros((112, HEAD_DIM), jnp.float32)], axis=0).T
        corr_cols[d * rows : (d + 1) * rows] = square[0:rows].astype(jnp.bfloat16)

    near[1].wait_recv()
    far[1].start()
    send_heads(4, 2, 2)


    def round_terms(start, count):
        for r in range(start, start + count):
            part = slice(r * rows, (r + 1) * rows)
            terms[r, 0] = (total[0, part] * scaling).astype(jnp.bfloat16)
            terms[r, 1] = total[1, part].astype(jnp.bfloat16)

    def term_copy(r, distance, d):
        return pltpu.make_async_remote_copy(
            src_ref=terms.at[r],
            dst_ref=arrived.at[distance, h],
            send_sem=send_sem.at[6],
            recv_sem=term_sem.at[distance],
            device_id=(at(-distance), d),
            device_id_type=MESH,
        )

    pass_back = pltpu.make_async_remote_copy(
        src_ref=terms.at[0:half],
        dst_ref=far_terms,
        send_sem=send_sem.at[7],
        recv_sem=far_term_sem,
        device_id=(at(-2), h),
        device_id_type=MESH,
    )

    def send_dq(i, count):
        cols = slice(i * HEAD_DIM, (i + count) * HEAD_DIM)
        target = dq_hbm.at[:, lanes_at(h * width + i * HEAD_DIM, count * HEAD_DIM)]

        def send_part(off, carry):
            d = other(off)
            pltpu.make_async_remote_copy(
                src_ref=dq_out.at[rows_at(d * rows, rows), cols],
                dst_ref=target,
                send_sem=send_sem.at[5],
                recv_sem=dq_sem,
                device_id=(p, d),
                device_id_type=MESH,
            ).start()
            return carry

        lax.fori_loop(1, devices, send_part, 0)
        pltpu.make_async_copy(dq_out.at[mine, cols], target, dq_sem).start()

    def send_half(i, count, late):
        cols = slice(i * HEAD_DIM, (i + count) * HEAD_DIM)
        target = dq_hbm.at[:, lanes_at(h * width + i * HEAD_DIM, count * HEAD_DIM)]

        def send_part(d, carry):
            source = dq_out.at[rows_at(d * rows, rows), cols]

            @pl.when(d != h)
            def _():
                pltpu.make_async_remote_copy(
                    src_ref=source,
                    dst_ref=target,
                    send_sem=send_sem.at[5],
                    recv_sem=dq_sem,
                    device_id=(p, d),
                    device_id_type=MESH,
                ).start()

            @pl.when(d == h)
            def _():
                pltpu.make_async_copy(source, target, dq_sem).start()

            return carry

        lax.fori_loop(late * half, (late + 1) * half, send_part, 0)

    reach = WINDOW * BLOCK
    held_scores, held_grads = (scores_a, scores_b), (grads_a, grads_b)
    lane = lax.broadcasted_iota(jnp.int32, (BLOCK, HEAD_DIM), 1)

    def operands(late, i):
        query_rows = rows_at(late * BLOCK, BLOCK)
        key_rows = rows_at(late * BLOCK, reach)
        heads = [lanes_at((i + n) * HEAD_DIM, HEAD_DIM) for n in range(2)]
        return query_rows, key_rows, heads

    def products(slot, late, i):
        query_rows, key_rows, heads = operands(late, i)
        q = jnp.concatenate([qg[0, query_rows, cols] for cols in heads], axis=0)
        g = jnp.concatenate([qg[1, query_rows, cols] for cols in heads], axis=0)
        corr = corr_cols[query_rows, :].astype(jnp.float32)
        corr = jnp.concatenate(
            [
                jnp.where((lane == i + n) | (lane == i + n + 8), corr, 0.0).astype(jnp.bfloat16)
                for n in range(2)
            ],
            axis=0,
        )
        held_scores[slot][...] = contract_last(k_band[key_rows, :], q)
        held_grads[slot][...] = contract_last(
            v_band[key_rows, :], jnp.concatenate([g, corr], axis=1)
        )

    def returns(slot, late, i):
        query_rows, key_rows, heads = operands(late, i)
        q = jnp.concatenate([qg[0, query_rows, cols] for cols in heads], axis=0)
        g = jnp.concatenate([qg[1, query_rows, cols] for cols in heads], axis=0)
        score = held_scores[slot][...]
        grads = held_grads[slot][...]
        first = first_ref[2 * p + late]
        tiles = [score[t * BLOCK : (t + 1) * BLOCK] for t in range(WINDOW)]
        biases = [
            jnp.where(first <= 2 * p + late - 3 + t, 0.0, -FAR).astype(jnp.float32)
            for t in range(WINDOW)
        ]
        peak = None
        for t in range(WINDOW):
            top = jnp.max(tiles[t], axis=0, keepdims=True) + biases[t]
            peak = top if peak is None else jnp.maximum(peak, top)
        level = peak * to_exp2
        weights = [
            jnp.exp2(tiles[t] * to_exp2 - (level - biases[t])) for t in range(WINDOW)
        ]
        weights = jnp.concatenate(weights, axis=0)
        probs = weights * (1.0 / jnp.sum(weights, axis=0, keepdims=True))
        grad_scores = (probs * grads).astype(jnp.bfloat16)
        total[0, key_rows, :] += jnp.dot(grad_scores, q, preferred_element_type=jnp.float32)
        total[1, key_rows, :] += jnp.dot(
            probs.astype(jnp.bfloat16), g, preferred_element_type=jnp.float32
        )
        dq_turned = jnp.dot(
            k_turned[:, lanes_at(late * BLOCK, reach)],
            grad_scores,
            preferred_element_type=jnp.float32,
        )
        dq = (dq_turned * scaling).T.astype(jnp.bfloat16)
        for n in range(2):
            dq_out[query_rows, heads[n]] = dq[n * BLOCK : (n + 1) * BLOCK]

    wait_heads(0, 2, 0)
    products(0, 1, 0)
    returns(0, 1, 0)
    far[0].wait_recv()
    far[1].wait_recv()
    turn(0)
    products(1, 0, 0)
    wait_heads(2, 2, 1)
    products(0, 1, 2)
    returns(1, 0, 0)
    products(1, 0, 2)
    returns(0, 1, 2)
    send_dq(0, 2)
    returns(1, 0, 2)
    send_dq(2, 2)
    wait_heads(4, 2, 2)
    products(0, 0, 4)
    products(1, 1, 4)
    returns(0, 0, 4)
    round_terms(0, half)
    pass_back.start()
    send_half(4, 2, 0)
    returns(1, 1, 4)

    round_terms(half, devices)

    def send_near(off, carry):
        d = other(off)
        term_copy(half + d, 1, d).start()
        return carry

    lax.fori_loop(0, devices, send_near, 0)
    send_half(4, 2, 1)
    def send_own(d, carry):
        source = terms.at[half + devices + d]

        @pl.when(d != h)
        def _():
            term_copy(half + devices + d, 0, d).start()

        @pl.when(d == h)
        def _():
            pltpu.make_async_copy(source, arrived.at[0, h], term_sem.at[0]).start()

        return carry

    round_terms(half + devices, half)
    lax.fori_loop(0, half, send_own, 0)
    pass_back.wait_recv()
    for r in range(half):
        at_row = half + devices + half + r
        part = slice(at_row * rows, (at_row + 1) * rows)
        terms[at_row, 0] = (
            total[0, part] * scaling + far_terms[r, 0].astype(jnp.float32)
        ).astype(jnp.bfloat16)
        terms[at_row, 1] = (total[1, part] + far_terms[r, 1].astype(jnp.float32)).astype(
            jnp.bfloat16
        )
    lax.fori_loop(half, devices, send_own, 0)

    pltpu.make_async_copy(arrived.at[0], arrived.at[0], term_sem.at[0]).wait()
    pltpu.make_async_copy(arrived.at[1], arrived.at[1], term_sem.at[1]).wait()
    for d in range(devices):
        cols = slice(d * HEAD_DIM, (d + 1) * HEAD_DIM)
        for index in range(2):
            held = arrived[0, d, index].astype(jnp.float32)
            more = arrived[1, d, index].astype(jnp.float32)
            dkv_ref[index, :, cols] = (held + more).astype(jnp.bfloat16)
    pltpu.make_async_copy(dq_hbm, dq_hbm, dq_sem).wait()

    most = span - rows

    def left(view, index):
        pltpu.make_async_copy(view, view, send_sem.at[index]).wait()

    left(k_band.at[0 : 2 * most], 0)
    left(corr_in.at[0 : devices - 1], 1)
    left(qg.at[:, 0:most], 2)
    left(k_band.at[0 : 2 * span], 3)
    left(k_band.at[0 : 2 * BLOCK], 4)
    pass_back.wait_send()
    left(dq_out.at[0:most], 5)
    left(terms.at[0 : 2 * devices - 1], 6)


def finish(pieces, dq, dkv, dq_hbm, dk_hbm, dv_hbm, held, held_kv, in_sem, out_sem):
    rows = held.shape[0] // pieces
    legs = []
    for n in range(pieces):
        part = slice(n * rows, (n + 1) * rows)
        legs.append((dq.at[part], held.at[part], dq_hbm.at[part]))
    legs.append((dkv.at[0], held_kv.at[0], dk_hbm))
    legs.append((dkv.at[1], held_kv.at[1], dv_hbm))
    loads, stores = [], []
    for n, (source, between, target) in enumerate(legs):
        loads.append(pltpu.make_async_copy(source, between, in_sem.at[n]))
        stores.append(pltpu.make_async_copy(between, target, out_sem.at[n]))
        loads[n].start()
    for n in range(len(legs)):
        loads[n].wait()
        stores[n].start()
    for n in range(len(legs)):
        stores[n].wait()


def solution(mesh):
    parts = mesh.shape["ctx"]
    devices = mesh.shape["head"]
    rows = 2 * BLOCK // devices

    def local(queries, keys, values, outputs, grad_out, first_block):
        group = queries.shape[1] // keys.shape[1]
        hbm = pl.BlockSpec(memory_space=pl.ANY)
        vmem = pl.BlockSpec(memory_space=pltpu.VMEM)
        low, full = jnp.bfloat16, jnp.float32
        dma = pltpu.SemaphoreType.DMA
        width = queries.shape[1] // devices
        pieces = 4
        band = 5 * BLOCK
        dq, dkv = pl.pallas_call(
            functools.partial(kernel, parts, devices, group),
            out_shape=(
                jax.ShapeDtypeStruct(queries.shape, low),
                jax.ShapeDtypeStruct((2, *keys.shape), low),
            ),
            in_specs=[hbm] * 5 + [pl.BlockSpec(memory_space=pltpu.SMEM)],
            out_specs=(hbm, vmem),
            scratch_shapes=[
                pltpu.VMEM(queries.shape, low),
                pltpu.VMEM(grad_out.shape, low),
                pltpu.VMEM(outputs.shape, low),
                pltpu.VMEM((devices, 16, HEAD_DIM), low),
                pltpu.VMEM((devices, 16, HEAD_DIM), low),
                pltpu.VMEM((2 * BLOCK, HEAD_DIM), low),
                pltpu.VMEM((2, 2 * BLOCK, width), low),
                pltpu.VMEM((band, HEAD_DIM), low),
                pltpu.VMEM((band, 2 * HEAD_DIM), low),
                pltpu.VMEM((HEAD_DIM, band), low),
                pltpu.VMEM((WINDOW * BLOCK, 2 * BLOCK), full),
                pltpu.VMEM((WINDOW * BLOCK, 2 * BLOCK), full),
                pltpu.VMEM((WINDOW * BLOCK, 2 * BLOCK), full),
                pltpu.VMEM((WINDOW * BLOCK, 2 * BLOCK), full),
                pltpu.VMEM((2, band, HEAD_DIM), full),
                pltpu.VMEM((2 * BLOCK, width), low),
                pltpu.VMEM((band // rows, 2, rows, HEAD_DIM), low),
                pltpu.VMEM((devices // 2, 2, rows, HEAD_DIM), low),
                pltpu.VMEM((2, devices, 2, rows, HEAD_DIM), low),
                dma((3,)),
                dma((2,)),
                dma((2,)),
                dma((2,)),
                dma,
                dma((3,)),
                dma,
                dma((2,)),
                dma,
                dma((8,)),
            ],
            compiler_params=pltpu.CompilerParams(
                collective_id=0,
                has_side_effects=True,
                vmem_limit_bytes=63 * 1024 * 1024,
            ),
            cost_estimate=pl.CostEstimate(
                flops=48 * 5 * 2 * 256 * 256 * 128, bytes_accessed=8_000_000, transcendentals=0
            ),
        )(queries, keys, values, outputs, grad_out, first_block)
        return pl.pallas_call(
            functools.partial(finish, pieces),
            out_shape=(
                jax.ShapeDtypeStruct(queries.shape, low),
                jax.ShapeDtypeStruct(keys.shape, low),
                jax.ShapeDtypeStruct(values.shape, low),
            ),
            in_specs=[hbm] * 2,
            out_specs=(hbm,) * 3,
            scratch_shapes=[
                pltpu.VMEM(queries.shape, low),
                pltpu.VMEM((2, *keys.shape), low),
                dma((pieces + 2,)),
                dma((pieces + 2,)),
            ],
            compiler_params=pltpu.CompilerParams(vmem_limit_bytes=63 * 1024 * 1024),
        )(dq, dkv)

    placed = P(("ctx", "head"), None)
    return jax.shard_map(
        local,
        mesh=mesh,
        in_specs=(placed,) * 5 + (P(),),
        out_specs=(placed,) * 3,
        check_vma=False,
    )
```

```python
import functools
import math

import jax
import jax.numpy as jnp
from jax import lax
from jax.experimental import pallas as pl
from jax.experimental.pallas import tpu as pltpu
from jax.sharding import PartitionSpec as P

HEAD_DIM = 128
BLOCK = 256
WINDOW = 4
MESH = pl.DeviceIdType.MESH
FAR = 1e30


def contract_last(a, b):
    return lax.dot_general(a, b, (((1,), (1,)), ((), ())), preferred_element_type=jnp.float32)


def kernel(
    parts,
    devices,
    group,
    q_hbm,
    k_hbm,
    v_hbm,
    o_hbm,
    g_hbm,
    first_ref,
    dq_hbm,
    dkv_ref,
    q_own,
    g_own,
    o_own,
    corr_out,
    corr_in,
    corr_cols,
    qg,
    k_band,
    v_band,
    k_turned,
    total,
    dq_out,
    terms,
    far_terms,
    arrived,
    load_sem,
    kv_sem,
    near_sem,
    far_sem,
    corr_sem,
    qg_sem,
    dq_sem,
    term_sem,
    far_term_sem,
    send_sem,
):
    rows = 2 * BLOCK // devices
    half = devices // 2
    width = group * HEAD_DIM
    span = 2 * BLOCK
    own = 3 * BLOCK
    scaling = HEAD_DIM ** (-0.5)
    to_exp2 = scaling * math.log2(math.e)
    p = lax.axis_index("ctx")
    h = lax.axis_index("head")

    def at(shift):
        return lax.rem(p + shift + parts, parts)

    def other(off):
        return lax.rem(h + off, devices)

    barrier = pltpu.get_barrier_semaphore()

    def greet_row(off, carry):
        pl.semaphore_signal(barrier, inc=1, device_id=(p, other(off)), device_id_type=MESH)
        return carry

    lax.fori_loop(1, devices, greet_row, 0)
    has_earlier, has_later = p >= 1, p <= parts - 2
    has_second_earlier, has_second_later = p >= 2, p <= parts - 3
    for shift, exists in ((1, has_later), (-1, has_earlier)):

        @pl.when(exists)
        def _():
            def greet_near(off, carry):
                pl.semaphore_signal(
                    barrier, inc=1, device_id=(at(shift), other(off)), device_id_type=MESH
                )
                return carry

            lax.fori_loop(0, devices, greet_near, 0)

    for shift, exists in ((2, has_second_later), (-2, has_second_earlier)):

        @pl.when(exists)
        def _():
            pl.semaphore_signal(barrier, inc=1, device_id=(at(shift), h), device_id_type=MESH)

    load_q = pltpu.make_async_copy(q_hbm, q_own, load_sem.at[0])
    load_g = pltpu.make_async_copy(g_hbm, g_own, load_sem.at[1])
    load_o = pltpu.make_async_copy(o_hbm, o_own, load_sem.at[2])
    load_q.start()
    load_g.start()
    load_o.start()

    @pl.when(p == 0)
    def _():
        k_band[BLOCK:own] = jnp.zeros((2 * BLOCK, HEAD_DIM), jnp.bfloat16)
        v_band[BLOCK:own, 0:HEAD_DIM] = jnp.zeros((2 * BLOCK, HEAD_DIM), jnp.bfloat16)

    @pl.when(p <= 1)
    def _():
        k_band[0:BLOCK] = jnp.zeros((BLOCK, HEAD_DIM), jnp.bfloat16)
        v_band[0:BLOCK, 0:HEAD_DIM] = jnp.zeros((BLOCK, HEAD_DIM), jnp.bfloat16)

    @pl.when(p == parts - 1)
    def _():
        arrived[1] = jnp.zeros((devices, 2, rows, HEAD_DIM), jnp.bfloat16)

    @pl.when(p >= parts - 2)
    def _():
        far_terms[...] = jnp.zeros((half, 2, rows, HEAD_DIM), jnp.bfloat16)

    after = parts - 1 - p
    neighbours = (p + parts - 1) // parts + (after + parts - 1) // parts
    seconds = (p + parts - 2) // parts + (after + parts - 2) // parts
    pl.semaphore_wait(barrier, devices - 1 + devices * neighbours + seconds)

    def rows_at(start, count):
        return pl.ds(pl.multiple_of(start, 64), count)

    def lanes_at(start, count):
        return pl.ds(pl.multiple_of(start, HEAD_DIM), count)

    mine = rows_at(h * rows, rows)
    mine_kv = rows_at(own + h * rows, rows)

    for index, source, band in ((0, k_hbm, k_band), (1, v_hbm, v_band)):

        def send_kv(off, carry):
            d = other(off)
            pltpu.make_async_remote_copy(
                src_ref=source.at[:, lanes_at(d * HEAD_DIM, HEAD_DIM)],
                dst_ref=band.at[mine_kv, 0:HEAD_DIM],
                send_sem=send_sem.at[0],
                recv_sem=kv_sem.at[index],
                device_id=(p, d),
                device_id_type=MESH,
            ).start()
            return carry

        lax.fori_loop(1, devices, send_kv, 0)
        pltpu.make_async_copy(
            source.at[:, lanes_at(h * HEAD_DIM, HEAD_DIM)], band.at[mine_kv, 0:HEAD_DIM], kv_sem.at[index]
        ).start()

    def send_heads(i, count, sem):
        for index, source in ((0, q_own), (1, g_own)):

            def send_part(off, carry):
                d = other(off)
                pltpu.make_async_remote_copy(
                    src_ref=source.at[:, lanes_at(d * width + i * HEAD_DIM, count * HEAD_DIM)],
                    dst_ref=qg.at[index, mine, lanes_at(i * HEAD_DIM, count * HEAD_DIM)],
                    send_sem=send_sem.at[2],
                    recv_sem=qg_sem.at[sem],
                    device_id=(p, d),
                    device_id_type=MESH,
                ).start()
                return carry

            lax.fori_loop(1, devices, send_part, 0)
            pltpu.make_async_copy(
                source.at[:, lanes_at(h * width + i * HEAD_DIM, count * HEAD_DIM)],
                qg.at[index, mine, lanes_at(i * HEAD_DIM, count * HEAD_DIM)],
                qg_sem.at[sem],
            ).start()

    def wait_heads(i, count, sem):
        part = qg.at[:, :, i * HEAD_DIM : (i + count) * HEAD_DIM]
        pltpu.make_async_copy(part, part, qg_sem.at[sem]).wait()

    load_q.wait()
    load_g.wait()
    send_heads(0, 2, 0)


    load_o.wait()
    row_of = lax.broadcasted_iota(jnp.int32, (16, width), 0)
    col_of = lax.broadcasted_iota(jnp.int32, (16, width), 1)
    pick = jnp.where((row_of % 8) == col_of // HEAD_DIM, 1.0, 0.0).astype(jnp.bfloat16)
    upper = lax.broadcasted_iota(jnp.int32, (16, rows), 0) < 8
    corr_out[...] = jnp.zeros_like(corr_out)
    for d in range(devices):
        cols = slice(d * width, (d + 1) * width)
        product = g_own[:, cols].astype(jnp.float32) * o_own[:, cols].astype(jnp.float32)
        high = product.astype(jnp.bfloat16)
        low = (product - high.astype(jnp.float32)).astype(jnp.bfloat16)
        corr = contract_last(pick, high) + contract_last(pick, low)
        corr_high = corr.astype(jnp.bfloat16).astype(jnp.float32)
        corr_out[d, :, 0:rows] = jnp.where(upper, corr_high, corr - corr_high).astype(jnp.bfloat16)

    def send_corr(off, carry):
        d = other(off)
        pltpu.make_async_remote_copy(
            src_ref=corr_out.at[d],
            dst_ref=corr_in.at[h],
            send_sem=send_sem.at[1],
            recv_sem=corr_sem,
            device_id=(p, d),
            device_id_type=MESH,
        ).start()
        return carry

    lax.fori_loop(1, devices, send_corr, 0)
    pltpu.make_async_copy(corr_out.at[h], corr_in.at[h], corr_sem).start()
    total[...] = jnp.zeros_like(total)
    v_band[:, HEAD_DIM:] = jnp.full((5 * BLOCK, HEAD_DIM), -1.0, jnp.bfloat16)


    near, far = [], []
    for index, band in ((0, k_band), (1, v_band)):
        held = band.at[own : own + span, 0:HEAD_DIM]
        pltpu.make_async_copy(held, held, kv_sem.at[index]).wait()
        near.append(
            pltpu.make_async_remote_copy(
                src_ref=held,
                dst_ref=band.at[BLOCK : BLOCK + span, 0:HEAD_DIM],
                send_sem=send_sem.at[3],
                recv_sem=near_sem.at[index],
                device_id=(at(1), h),
                device_id_type=MESH,
            )
        )
        pl.when(has_later)(near[index].start)
        far.append(
            pltpu.make_async_remote_copy(
                src_ref=band.at[2 * BLOCK : 3 * BLOCK, 0:HEAD_DIM],
                dst_ref=band.at[0:BLOCK, 0:HEAD_DIM],
                send_sem=send_sem.at[4],
                recv_sem=far_sem.at[index],
                device_id=(at(1), h),
                device_id_type=MESH,
            )
        )
    send_heads(2, 2, 1)

    def turn(block):
        part = slice(block * BLOCK, (block + 1) * BLOCK)
        k_turned[:, part] = k_band[part].astype(jnp.float32).T.astype(jnp.bfloat16)

    turn(3)
    turn(4)
    pl.when(has_earlier)(near[0].wait_recv)
    pl.when(has_earlier & has_later)(far[0].start)
    turn(1)
    turn(2)

    pltpu.make_async_copy(corr_in, corr_in, corr_sem).wait()
    for d in range(devices):
        piece = corr_in[d].astype(jnp.float32)
        square = jnp.concatenate([piece, jnp.zeros((112, HEAD_DIM), jnp.float32)], axis=0).T
        corr_cols[d * rows : (d + 1) * rows] = square[0:rows].astype(jnp.bfloat16)

    pl.when(has_earlier)(near[1].wait_recv)
    pl.when(has_earlier & has_later)(far[1].start)
    send_heads(4, 2, 2)


    def round_terms(start, count):
        for r in range(start, start + count):
            part = slice(r * rows, (r + 1) * rows)
            terms[r, 0] = (total[0, part] * scaling).astype(jnp.bfloat16)
            terms[r, 1] = total[1, part].astype(jnp.bfloat16)

    def term_copy(r, distance, d):
        return pltpu.make_async_remote_copy(
            src_ref=terms.at[r],
            dst_ref=arrived.at[distance, h],
            send_sem=send_sem.at[6 + 2 * distance],
            recv_sem=term_sem.at[distance],
            device_id=(at(-distance), d),
            device_id_type=MESH,
        )

    pass_back = pltpu.make_async_remote_copy(
        src_ref=terms.at[0:half],
        dst_ref=far_terms,
        send_sem=send_sem.at[7],
        recv_sem=far_term_sem,
        device_id=(at(-2), h),
        device_id_type=MESH,
    )

    def send_dq(i, count):
        cols = slice(i * HEAD_DIM, (i + count) * HEAD_DIM)
        target = dq_hbm.at[:, lanes_at(h * width + i * HEAD_DIM, count * HEAD_DIM)]

        def send_part(off, carry):
            d = other(off)
            pltpu.make_async_remote_copy(
                src_ref=dq_out.at[rows_at(d * rows, rows), cols],
                dst_ref=target,
                send_sem=send_sem.at[5],
                recv_sem=dq_sem,
                device_id=(p, d),
                device_id_type=MESH,
            ).start()
            return carry

        lax.fori_loop(1, devices, send_part, 0)
        pltpu.make_async_copy(dq_out.at[mine, cols], target, dq_sem).start()

    def send_half(i, count, late):
        cols = slice(i * HEAD_DIM, (i + count) * HEAD_DIM)
        target = dq_hbm.at[:, lanes_at(h * width + i * HEAD_DIM, count * HEAD_DIM)]

        def send_part(d, carry):
            source = dq_out.at[rows_at(d * rows, rows), cols]

            @pl.when(d != h)
            def _():
                pltpu.make_async_remote_copy(
                    src_ref=source,
                    dst_ref=target,
                    send_sem=send_sem.at[5],
                    recv_sem=dq_sem,
                    device_id=(p, d),
                    device_id_type=MESH,
                ).start()

            @pl.when(d == h)
            def _():
                pltpu.make_async_copy(source, target, dq_sem).start()

            return carry

        lax.fori_loop(late * half, (late + 1) * half, send_part, 0)

    reach = WINDOW * BLOCK
    lane = lax.broadcasted_iota(jnp.int32, (BLOCK, HEAD_DIM), 1)

    def pair(k, carry):
        late = ((k + 1) % 2) * (1 - k // 4) + (k // 4) * (k % 2)
        i = 2 * (k // 2)

        @pl.when(k == 1)
        def _():
            pl.when(has_second_earlier)(far[0].wait_recv)
            pl.when(has_second_earlier)(far[1].wait_recv)
            turn(0)

        @pl.when(k == 2)
        def _():
            wait_heads(2, 2, 1)

        @pl.when(k == 4)
        def _():
            wait_heads(4, 2, 2)

        query_rows = rows_at(late * BLOCK, BLOCK)
        key_rows = rows_at(late * BLOCK, reach)
        heads = [lanes_at((i + n) * HEAD_DIM, HEAD_DIM) for n in range(2)]
        q = jnp.concatenate([qg[0, query_rows, cols] for cols in heads], axis=0)
        g = jnp.concatenate([qg[1, query_rows, cols] for cols in heads], axis=0)
        corr = corr_cols[query_rows, :].astype(jnp.float32)
        corr = jnp.concatenate(
            [
                jnp.where((lane == i + n) | (lane == i + n + 8), corr, 0.0).astype(jnp.bfloat16)
                for n in range(2)
            ],
            axis=0,
        )
        score = contract_last(k_band[key_rows, :], q)
        grads = contract_last(v_band[key_rows, :], jnp.concatenate([g, corr], axis=1))
        first = first_ref[2 * p + late]
        tiles = [score[t * BLOCK : (t + 1) * BLOCK] for t in range(WINDOW)]
        biases = [
            jnp.where(first <= 2 * p + late - 3 + t, 0.0, -FAR).astype(jnp.float32)
            for t in range(WINDOW)
        ]
        peak = None
        for t in range(WINDOW):
            top = jnp.max(tiles[t], axis=0, keepdims=True) + biases[t]
            peak = top if peak is None else jnp.maximum(peak, top)
        level = peak * to_exp2
        weights = [
            jnp.exp2(tiles[t] * to_exp2 - (level - biases[t])) for t in range(WINDOW)
        ]
        weights = jnp.concatenate(weights, axis=0)
        probs = weights * (1.0 / jnp.sum(weights, axis=0, keepdims=True))
        grad_scores = (probs * grads).astype(jnp.bfloat16)
        total[0, key_rows, :] += jnp.dot(grad_scores, q, preferred_element_type=jnp.float32)
        total[1, key_rows, :] += jnp.dot(
            probs.astype(jnp.bfloat16), g, preferred_element_type=jnp.float32
        )
        dq_turned = jnp.dot(
            k_turned[:, lanes_at(late * BLOCK, reach)],
            grad_scores,
            preferred_element_type=jnp.float32,
        )
        dq = (dq_turned * scaling).T.astype(jnp.bfloat16)
        for n in range(2):
            dq_out[query_rows, heads[n]] = dq[n * BLOCK : (n + 1) * BLOCK]

        @pl.when(k == 1)
        def _():
            send_dq(0, 2)

        @pl.when(k == 3)
        def _():
            send_dq(2, 2)

        @pl.when(k == 4)
        def _():
            round_terms(0, half)
            pl.when(has_second_earlier)(pass_back.start)
            send_half(4, 2, 0)

        return carry

    wait_heads(0, 2, 0)
    lax.fori_loop(0, group, pair, 0)

    round_terms(half, devices)

    def send_near(off, carry):
        d = other(off)
        term_copy(half + d, 1, d).start()
        return carry

    @pl.when(has_earlier)
    def _():
        lax.fori_loop(0, devices, send_near, 0)

    send_half(4, 2, 1)
    def send_own(d, carry):
        source = terms.at[half + devices + d]

        @pl.when(d != h)
        def _():
            term_copy(half + devices + d, 0, d).start()

        @pl.when(d == h)
        def _():
            pltpu.make_async_copy(source, arrived.at[0, h], term_sem.at[0]).start()

        return carry

    round_terms(half + devices, half)
    lax.fori_loop(0, half, send_own, 0)
    pl.when(has_second_later)(pass_back.wait_recv)
    for r in range(half):
        at_row = half + devices + half + r
        part = slice(at_row * rows, (at_row + 1) * rows)
        terms[at_row, 0] = (
            total[0, part] * scaling + far_terms[r, 0].astype(jnp.float32)
        ).astype(jnp.bfloat16)
        terms[at_row, 1] = (total[1, part] + far_terms[r, 1].astype(jnp.float32)).astype(
            jnp.bfloat16
        )
    lax.fori_loop(half, devices, send_own, 0)

    pltpu.make_async_copy(arrived.at[0], arrived.at[0], term_sem.at[0]).wait()
    pl.when(has_later)(
        pltpu.make_async_copy(arrived.at[1], arrived.at[1], term_sem.at[1]).wait
    )
    for d in range(devices):
        cols = slice(d * HEAD_DIM, (d + 1) * HEAD_DIM)
        for index in range(2):
            held = arrived[0, d, index].astype(jnp.float32)
            more = arrived[1, d, index].astype(jnp.float32)
            dkv_ref[index, :, cols] = (held + more).astype(jnp.bfloat16)
    pltpu.make_async_copy(dq_hbm, dq_hbm, dq_sem).wait()

    most = span - rows

    def left(view, index):
        pltpu.make_async_copy(view, view, send_sem.at[index]).wait()

    left(k_band.at[0 : 2 * most], 0)
    left(corr_in.at[0 : devices - 1], 1)
    left(qg.at[:, 0:most], 2)
    left(dq_out.at[0:most], 5)
    left(terms.at[0 : devices - 1], 6)

    @pl.when(has_later)
    def _():
        left(k_band.at[0 : 2 * span], 3)

    @pl.when(has_earlier & has_later)
    def _():
        left(k_band.at[0 : 2 * BLOCK], 4)

    @pl.when(has_earlier)
    def _():
        left(terms.at[0:devices], 8)

    pl.when(has_second_earlier)(pass_back.wait_send)


def finish(pieces, dq, dkv, dq_hbm, dk_hbm, dv_hbm, held, held_kv, in_sem, out_sem):
    rows = held.shape[0] // pieces
    legs = []
    for n in range(pieces):
        part = slice(n * rows, (n + 1) * rows)
        legs.append((dq.at[part], held.at[part], dq_hbm.at[part]))
    legs.append((dkv.at[0], held_kv.at[0], dk_hbm))
    legs.append((dkv.at[1], held_kv.at[1], dv_hbm))
    loads, stores = [], []
    for n, (source, between, target) in enumerate(legs):
        loads.append(pltpu.make_async_copy(source, between, in_sem.at[n]))
        stores.append(pltpu.make_async_copy(between, target, out_sem.at[n]))
        loads[n].start()
    for n in range(len(legs)):
        loads[n].wait()
        stores[n].start()
    for n in range(len(legs)):
        stores[n].wait()


def solution(mesh):
    parts = mesh.shape["ctx"]
    devices = mesh.shape["head"]
    rows = 2 * BLOCK // devices

    def local(queries, keys, values, outputs, grad_out, first_block):
        group = queries.shape[1] // keys.shape[1]
        hbm = pl.BlockSpec(memory_space=pl.ANY)
        vmem = pl.BlockSpec(memory_space=pltpu.VMEM)
        low, full = jnp.bfloat16, jnp.float32
        dma = pltpu.SemaphoreType.DMA
        width = queries.shape[1] // devices
        pieces = 4
        band = 5 * BLOCK
        dq, dkv = pl.pallas_call(
            functools.partial(kernel, parts, devices, group),
            out_shape=(
                jax.ShapeDtypeStruct(queries.shape, low),
                jax.ShapeDtypeStruct((2, *keys.shape), low),
            ),
            in_specs=[hbm] * 5 + [pl.BlockSpec(memory_space=pltpu.SMEM)],
            out_specs=(hbm, vmem),
            scratch_shapes=[
                pltpu.VMEM(queries.shape, low),
                pltpu.VMEM(grad_out.shape, low),
                pltpu.VMEM(outputs.shape, low),
                pltpu.VMEM((devices, 16, HEAD_DIM), low),
                pltpu.VMEM((devices, 16, HEAD_DIM), low),
                pltpu.VMEM((2 * BLOCK, HEAD_DIM), low),
                pltpu.VMEM((2, 2 * BLOCK, width), low),
                pltpu.VMEM((band, HEAD_DIM), low),
                pltpu.VMEM((band, 2 * HEAD_DIM), low),
                pltpu.VMEM((HEAD_DIM, band), low),
                pltpu.VMEM((2, band, HEAD_DIM), full),
                pltpu.VMEM((2 * BLOCK, width), low),
                pltpu.VMEM((band // rows, 2, rows, HEAD_DIM), low),
                pltpu.VMEM((devices // 2, 2, rows, HEAD_DIM), low),
                pltpu.VMEM((2, devices, 2, rows, HEAD_DIM), low),
                dma((3,)),
                dma((2,)),
                dma((2,)),
                dma((2,)),
                dma,
                dma((3,)),
                dma,
                dma((2,)),
                dma,
                dma((9,)),
            ],
            compiler_params=pltpu.CompilerParams(
                collective_id=0,
                has_side_effects=True,
                vmem_limit_bytes=63 * 1024 * 1024,
            ),
            cost_estimate=pl.CostEstimate(
                flops=48 * 5 * 2 * 256 * 256 * 128, bytes_accessed=8_000_000, transcendentals=0
            ),
        )(queries, keys, values, outputs, grad_out, first_block)
        return pl.pallas_call(
            functools.partial(finish, pieces),
            out_shape=(
                jax.ShapeDtypeStruct(queries.shape, low),
                jax.ShapeDtypeStruct(keys.shape, low),
                jax.ShapeDtypeStruct(values.shape, low),
            ),
            in_specs=[hbm] * 2,
            out_specs=(hbm,) * 3,
            scratch_shapes=[
                pltpu.VMEM(queries.shape, low),
                pltpu.VMEM((2, *keys.shape), low),
                dma((pieces + 2,)),
                dma((pieces + 2,)),
            ],
            compiler_params=pltpu.CompilerParams(vmem_limit_bytes=63 * 1024 * 1024),
        )(dq, dkv)

    placed = P(("ctx", "head"), None)
    return jax.shard_map(
        local,
        mesh=mesh,
        in_specs=(placed,) * 5 + (P(),),
        out_specs=(placed,) * 3,
        check_vma=False,
    )
```

```python
import functools
import math

import jax
import jax.numpy as jnp
from jax import lax
from jax.experimental import pallas as pl
from jax.experimental.pallas import tpu as pltpu
from jax.sharding import PartitionSpec as P

HEAD_DIM = 128
BLOCK = 256
WINDOW = 4
MESH = pl.DeviceIdType.MESH
FAR = 1e30


def contract_last(a, b):
    return lax.dot_general(a, b, (((1,), (1,)), ((), ())), preferred_element_type=jnp.float32)


def kernel(
    parts,
    devices,
    group,
    q_hbm,
    k_hbm,
    v_hbm,
    o_hbm,
    g_hbm,
    first_ref,
    dq_hbm,
    dkv_ref,
    q_own,
    g_own,
    o_own,
    corr_out,
    corr_in,
    corr_cols,
    qg,
    k_band,
    v_band,
    k_turned,
    total,
    dq_out,
    terms,
    far_terms,
    arrived,
    load_sem,
    kv_sem,
    near_sem,
    far_sem,
    corr_sem,
    qg_sem,
    dq_sem,
    term_sem,
    far_term_sem,
    send_sem,
):
    rows = 2 * BLOCK // devices
    half = devices // 2
    width = group * HEAD_DIM
    span = 2 * BLOCK
    own = 3 * BLOCK
    scaling = HEAD_DIM ** (-0.5)
    to_exp2 = scaling * math.log2(math.e)
    p = lax.axis_index("ctx")
    h = lax.axis_index("head")

    def at(shift):
        return lax.rem(p + shift + parts, parts)

    def other(off):
        return lax.rem(h + off, devices)

    barrier = pltpu.get_barrier_semaphore()

    def greet_row(off, carry):
        pl.semaphore_signal(barrier, inc=1, device_id=(p, other(off)), device_id_type=MESH)
        return carry

    lax.fori_loop(1, devices, greet_row, 0)
    has_earlier, has_later = p >= 1, p <= parts - 2
    has_second_earlier = p >= 2
    for shift, exists in ((1, has_later), (-1, has_earlier)):

        @pl.when(exists)
        def _():
            def greet_near(off, carry):
                pl.semaphore_signal(
                    barrier, inc=1, device_id=(at(shift), other(off)), device_id_type=MESH
                )
                return carry

            lax.fori_loop(0, devices, greet_near, 0)

    load_q = pltpu.make_async_copy(q_hbm, q_own, load_sem.at[0])
    load_g = pltpu.make_async_copy(g_hbm, g_own, load_sem.at[1])
    load_o = pltpu.make_async_copy(o_hbm, o_own, load_sem.at[2])
    load_q.start()
    load_g.start()
    load_o.start()

    @pl.when(p == 0)
    def _():
        k_band[BLOCK:own] = jnp.zeros((2 * BLOCK, HEAD_DIM), jnp.bfloat16)
        v_band[BLOCK:own, 0:HEAD_DIM] = jnp.zeros((2 * BLOCK, HEAD_DIM), jnp.bfloat16)

    @pl.when(p <= 1)
    def _():
        k_band[0:BLOCK] = jnp.zeros((BLOCK, HEAD_DIM), jnp.bfloat16)
        v_band[0:BLOCK, 0:HEAD_DIM] = jnp.zeros((BLOCK, HEAD_DIM), jnp.bfloat16)

    @pl.when(p == parts - 1)
    def _():
        arrived[1] = jnp.zeros((devices, 2, rows, HEAD_DIM), jnp.bfloat16)

    @pl.when((p == 0) | (p == parts - 1))
    def _():
        far_terms[...] = jnp.zeros((half, 2, rows, HEAD_DIM), jnp.bfloat16)

    after = parts - 1 - p
    neighbours = (p + parts - 1) // parts + (after + parts - 1) // parts
    pl.semaphore_wait(barrier, devices - 1 + devices * neighbours)

    def rows_at(start, count):
        return pl.ds(pl.multiple_of(start, 64), count)

    def lanes_at(start, count):
        return pl.ds(pl.multiple_of(start, HEAD_DIM), count)

    mine = rows_at(h * rows, rows)
    mine_kv = rows_at(own + h * rows, rows)

    for index, source, band in ((0, k_hbm, k_band), (1, v_hbm, v_band)):

        def send_kv(off, carry):
            d = other(off)
            pltpu.make_async_remote_copy(
                src_ref=source.at[:, lanes_at(d * HEAD_DIM, HEAD_DIM)],
                dst_ref=band.at[mine_kv, 0:HEAD_DIM],
                send_sem=send_sem.at[0],
                recv_sem=kv_sem.at[index],
                device_id=(p, d),
                device_id_type=MESH,
            ).start()
            return carry

        lax.fori_loop(1, devices, send_kv, 0)
        pltpu.make_async_copy(
            source.at[:, lanes_at(h * HEAD_DIM, HEAD_DIM)], band.at[mine_kv, 0:HEAD_DIM], kv_sem.at[index]
        ).start()

    def send_heads(i, count, sem):
        for index, source in ((0, q_own), (1, g_own)):

            def send_part(off, carry):
                d = other(off)
                pltpu.make_async_remote_copy(
                    src_ref=source.at[:, lanes_at(d * width + i * HEAD_DIM, count * HEAD_DIM)],
                    dst_ref=qg.at[index, mine, lanes_at(i * HEAD_DIM, count * HEAD_DIM)],
                    send_sem=send_sem.at[2],
                    recv_sem=qg_sem.at[sem],
                    device_id=(p, d),
                    device_id_type=MESH,
                ).start()
                return carry

            lax.fori_loop(1, devices, send_part, 0)
            pltpu.make_async_copy(
                source.at[:, lanes_at(h * width + i * HEAD_DIM, count * HEAD_DIM)],
                qg.at[index, mine, lanes_at(i * HEAD_DIM, count * HEAD_DIM)],
                qg_sem.at[sem],
            ).start()

    def wait_heads(i, count, sem):
        part = qg.at[:, :, i * HEAD_DIM : (i + count) * HEAD_DIM]
        pltpu.make_async_copy(part, part, qg_sem.at[sem]).wait()

    load_q.wait()
    load_g.wait()
    send_heads(0, 2, 0)


    load_o.wait()
    row_of = lax.broadcasted_iota(jnp.int32, (16, width), 0)
    col_of = lax.broadcasted_iota(jnp.int32, (16, width), 1)
    pick = jnp.where((row_of % 8) == col_of // HEAD_DIM, 1.0, 0.0).astype(jnp.bfloat16)
    upper = lax.broadcasted_iota(jnp.int32, (16, rows), 0) < 8
    corr_out[...] = jnp.zeros_like(corr_out)
    for d in range(devices):
        cols = slice(d * width, (d + 1) * width)
        product = g_own[:, cols].astype(jnp.float32) * o_own[:, cols].astype(jnp.float32)
        high = product.astype(jnp.bfloat16)
        low = (product - high.astype(jnp.float32)).astype(jnp.bfloat16)
        corr = contract_last(pick, high) + contract_last(pick, low)
        corr_high = corr.astype(jnp.bfloat16).astype(jnp.float32)
        corr_out[d, :, 0:rows] = jnp.where(upper, corr_high, corr - corr_high).astype(jnp.bfloat16)

    def send_corr(off, carry):
        d = other(off)
        pltpu.make_async_remote_copy(
            src_ref=corr_out.at[d],
            dst_ref=corr_in.at[h],
            send_sem=send_sem.at[1],
            recv_sem=corr_sem,
            device_id=(p, d),
            device_id_type=MESH,
        ).start()
        return carry

    lax.fori_loop(1, devices, send_corr, 0)
    pltpu.make_async_copy(corr_out.at[h], corr_in.at[h], corr_sem).start()
    total[...] = jnp.zeros_like(total)
    v_band[:, HEAD_DIM:] = jnp.full((5 * BLOCK, HEAD_DIM), -1.0, jnp.bfloat16)


    near, far = [], []
    for index, band in ((0, k_band), (1, v_band)):
        held = band.at[own : own + span, 0:HEAD_DIM]
        pltpu.make_async_copy(held, held, kv_sem.at[index]).wait()
        near.append(
            pltpu.make_async_remote_copy(
                src_ref=held,
                dst_ref=band.at[BLOCK : BLOCK + span, 0:HEAD_DIM],
                send_sem=send_sem.at[3],
                recv_sem=near_sem.at[index],
                device_id=(at(1), h),
                device_id_type=MESH,
            )
        )
        pl.when(has_later)(near[index].start)
        far.append(
            pltpu.make_async_remote_copy(
                src_ref=band.at[2 * BLOCK : 3 * BLOCK, 0:HEAD_DIM],
                dst_ref=band.at[0:BLOCK, 0:HEAD_DIM],
                send_sem=send_sem.at[4],
                recv_sem=far_sem.at[index],
                device_id=(at(1), h),
                device_id_type=MESH,
            )
        )
    send_heads(2, 2, 1)

    def turn(block):
        part = slice(block * BLOCK, (block + 1) * BLOCK)
        k_turned[:, part] = k_band[part].astype(jnp.float32).T.astype(jnp.bfloat16)

    turn(3)
    turn(4)
    pl.when(has_earlier)(near[0].wait_recv)
    pl.when(has_earlier & has_later)(far[0].start)
    turn(1)
    turn(2)

    pltpu.make_async_copy(corr_in, corr_in, corr_sem).wait()
    for d in range(devices):
        piece = corr_in[d].astype(jnp.float32)
        square = jnp.concatenate([piece, jnp.zeros((112, HEAD_DIM), jnp.float32)], axis=0).T
        corr_cols[d * rows : (d + 1) * rows] = square[0:rows].astype(jnp.bfloat16)

    pl.when(has_earlier)(near[1].wait_recv)
    pl.when(has_earlier & has_later)(far[1].start)
    send_heads(4, 2, 2)


    def round_terms(start, count):
        for r in range(start, start + count):
            part = slice(r * rows, (r + 1) * rows)
            terms[r, 0] = (total[0, part] * scaling).astype(jnp.bfloat16)
            terms[r, 1] = total[1, part].astype(jnp.bfloat16)

    def term_copy(r, distance, d):
        return pltpu.make_async_remote_copy(
            src_ref=terms.at[r],
            dst_ref=arrived.at[distance, h],
            send_sem=send_sem.at[6 + 2 * distance],
            recv_sem=term_sem.at[distance],
            device_id=(at(-distance), d),
            device_id_type=MESH,
        )

    pass_back = pltpu.make_async_remote_copy(
        src_ref=terms.at[0:half],
        dst_ref=far_terms,
        send_sem=send_sem.at[7],
        recv_sem=far_term_sem,
        device_id=(at(-1), h),
        device_id_type=MESH,
    )

    def send_dq(i, count):
        cols = slice(i * HEAD_DIM, (i + count) * HEAD_DIM)
        target = dq_hbm.at[:, lanes_at(h * width + i * HEAD_DIM, count * HEAD_DIM)]

        def send_part(off, carry):
            d = other(off)
            pltpu.make_async_remote_copy(
                src_ref=dq_out.at[rows_at(d * rows, rows), cols],
                dst_ref=target,
                send_sem=send_sem.at[5],
                recv_sem=dq_sem,
                device_id=(p, d),
                device_id_type=MESH,
            ).start()
            return carry

        lax.fori_loop(1, devices, send_part, 0)
        pltpu.make_async_copy(dq_out.at[mine, cols], target, dq_sem).start()

    def send_half(i, count, late):
        cols = slice(i * HEAD_DIM, (i + count) * HEAD_DIM)
        target = dq_hbm.at[:, lanes_at(h * width + i * HEAD_DIM, count * HEAD_DIM)]

        def send_part(d, carry):
            source = dq_out.at[rows_at(d * rows, rows), cols]

            @pl.when(d != h)
            def _():
                pltpu.make_async_remote_copy(
                    src_ref=source,
                    dst_ref=target,
                    send_sem=send_sem.at[5],
                    recv_sem=dq_sem,
                    device_id=(p, d),
                    device_id_type=MESH,
                ).start()

            @pl.when(d == h)
            def _():
                pltpu.make_async_copy(source, target, dq_sem).start()

            return carry

        lax.fori_loop(late * half, (late + 1) * half, send_part, 0)

    reach = WINDOW * BLOCK
    lane = lax.broadcasted_iota(jnp.int32, (BLOCK, HEAD_DIM), 1)

    def pair(k, carry):
        late = ((k + 1) % 2) * (1 - k // 4) + (k // 4) * (k % 2)
        i = 2 * (k // 2)

        @pl.when(k == 1)
        def _():
            pl.when(has_second_earlier)(far[0].wait_recv)
            pl.when(has_second_earlier)(far[1].wait_recv)
            turn(0)

        @pl.when(k == 2)
        def _():
            wait_heads(2, 2, 1)

        @pl.when(k == 4)
        def _():
            wait_heads(4, 2, 2)

        query_rows = rows_at(late * BLOCK, BLOCK)
        key_rows = rows_at(late * BLOCK, reach)
        heads = [lanes_at((i + n) * HEAD_DIM, HEAD_DIM) for n in range(2)]
        q = jnp.concatenate([qg[0, query_rows, cols] for cols in heads], axis=0)
        g = jnp.concatenate([qg[1, query_rows, cols] for cols in heads], axis=0)
        corr = corr_cols[query_rows, :].astype(jnp.float32)
        corr = jnp.concatenate(
            [
                jnp.where((lane == i + n) | (lane == i + n + 8), corr, 0.0).astype(jnp.bfloat16)
                for n in range(2)
            ],
            axis=0,
        )
        score = contract_last(k_band[key_rows, :], q)
        grads = contract_last(v_band[key_rows, :], jnp.concatenate([g, corr], axis=1))
        first = first_ref[2 * p + late]
        tiles = [score[t * BLOCK : (t + 1) * BLOCK] for t in range(WINDOW)]
        biases = [
            jnp.where(first <= 2 * p + late - 3 + t, 0.0, -FAR).astype(jnp.float32)
            for t in range(WINDOW)
        ]
        peak = None
        for t in range(WINDOW):
            top = jnp.max(tiles[t], axis=0, keepdims=True) + biases[t]
            peak = top if peak is None else jnp.maximum(peak, top)
        level = peak * to_exp2
        weights = [
            jnp.exp2(tiles[t] * to_exp2 - (level - biases[t])) for t in range(WINDOW)
        ]
        weights = jnp.concatenate(weights, axis=0)
        probs = weights * (1.0 / jnp.sum(weights, axis=0, keepdims=True))
        grad_scores = (probs * grads).astype(jnp.bfloat16)
        total[0, key_rows, :] += jnp.dot(grad_scores, q, preferred_element_type=jnp.float32)
        total[1, key_rows, :] += jnp.dot(
            probs.astype(jnp.bfloat16), g, preferred_element_type=jnp.float32
        )
        dq_turned = jnp.dot(
            k_turned[:, lanes_at(late * BLOCK, reach)],
            grad_scores,
            preferred_element_type=jnp.float32,
        )
        dq = (dq_turned * scaling).T.astype(jnp.bfloat16)
        for n in range(2):
            dq_out[query_rows, heads[n]] = dq[n * BLOCK : (n + 1) * BLOCK]

        @pl.when(k == 1)
        def _():
            send_dq(0, 2)

        @pl.when(k == 3)
        def _():
            send_dq(2, 2)

        @pl.when(k == 4)
        def _():
            round_terms(0, half)
            pl.when(has_second_earlier)(pass_back.start)
            send_half(4, 2, 0)

        return carry

    wait_heads(0, 2, 0)
    lax.fori_loop(0, group, pair, 0)

    def send_near(d, carry):
        term_copy(half + d, 1, d).start()
        return carry

    def send_own(off, carry):
        d = other(off)
        term_copy(half + devices + d, 0, d).start()
        return carry

    round_terms(half, half)

    @pl.when(has_earlier)
    def _():
        lax.fori_loop(0, half, send_near, 0)

    round_terms(half + devices, devices)
    lax.fori_loop(1, devices, send_own, 0)
    pltpu.make_async_copy(
        terms.at[half + devices + h], arrived.at[0, h], term_sem.at[0]
    ).start()
    send_half(4, 2, 1)

    pl.when(has_earlier & has_later)(pass_back.wait_recv)
    for r in range(half):
        at_row = devices + r
        part = slice(at_row * rows, (at_row + 1) * rows)
        terms[at_row, 0] = (
            total[0, part] * scaling + far_terms[r, 0].astype(jnp.float32)
        ).astype(jnp.bfloat16)
        terms[at_row, 1] = (total[1, part] + far_terms[r, 1].astype(jnp.float32)).astype(
            jnp.bfloat16
        )

    @pl.when(has_earlier)
    def _():
        lax.fori_loop(half, devices, send_near, 0)

    pltpu.make_async_copy(arrived.at[0], arrived.at[0], term_sem.at[0]).wait()
    pl.when(has_later)(
        pltpu.make_async_copy(arrived.at[1], arrived.at[1], term_sem.at[1]).wait
    )
    for d in range(devices):
        cols = slice(d * HEAD_DIM, (d + 1) * HEAD_DIM)
        for index in range(2):
            held = arrived[0, d, index].astype(jnp.float32)
            more = arrived[1, d, index].astype(jnp.float32)
            dkv_ref[index, :, cols] = (held + more).astype(jnp.bfloat16)
    pltpu.make_async_copy(dq_hbm, dq_hbm, dq_sem).wait()

    most = span - rows

    def left(view, index):
        pltpu.make_async_copy(view, view, send_sem.at[index]).wait()

    left(k_band.at[0 : 2 * most], 0)
    left(corr_in.at[0 : devices - 1], 1)
    left(qg.at[:, 0:most], 2)
    left(dq_out.at[0:most], 5)
    left(terms.at[0 : devices - 1], 6)

    @pl.when(has_later)
    def _():
        left(k_band.at[0 : 2 * span], 3)

    @pl.when(has_earlier & has_later)
    def _():
        left(k_band.at[0 : 2 * BLOCK], 4)

    @pl.when(has_earlier)
    def _():
        left(terms.at[0:devices], 8)

    pl.when(has_second_earlier)(pass_back.wait_send)


def finish(pieces, dq, dkv, dq_hbm, dk_hbm, dv_hbm, held, held_kv, in_sem, out_sem):
    rows = held.shape[0] // pieces
    legs = []
    for n in range(pieces):
        part = slice(n * rows, (n + 1) * rows)
        legs.append((dq.at[part], held.at[part], dq_hbm.at[part]))
    legs.append((dkv.at[0], held_kv.at[0], dk_hbm))
    legs.append((dkv.at[1], held_kv.at[1], dv_hbm))
    loads, stores = [], []
    for n, (source, between, target) in enumerate(legs):
        loads.append(pltpu.make_async_copy(source, between, in_sem.at[n]))
        stores.append(pltpu.make_async_copy(between, target, out_sem.at[n]))
        loads[n].start()
    for n in range(len(legs)):
        loads[n].wait()
        stores[n].start()
    for n in range(len(legs)):
        stores[n].wait()


def solution(mesh):
    parts = mesh.shape["ctx"]
    devices = mesh.shape["head"]
    rows = 2 * BLOCK // devices

    def local(queries, keys, values, outputs, grad_out, first_block):
        group = queries.shape[1] // keys.shape[1]
        hbm = pl.BlockSpec(memory_space=pl.ANY)
        vmem = pl.BlockSpec(memory_space=pltpu.VMEM)
        low, full = jnp.bfloat16, jnp.float32
        dma = pltpu.SemaphoreType.DMA
        width = queries.shape[1] // devices
        pieces = 4
        band = 5 * BLOCK
        dq, dkv = pl.pallas_call(
            functools.partial(kernel, parts, devices, group),
            out_shape=(
                jax.ShapeDtypeStruct(queries.shape, low),
                jax.ShapeDtypeStruct((2, *keys.shape), low),
            ),
            in_specs=[hbm] * 5 + [pl.BlockSpec(memory_space=pltpu.SMEM)],
            out_specs=(hbm, vmem),
            scratch_shapes=[
                pltpu.VMEM(queries.shape, low),
                pltpu.VMEM(grad_out.shape, low),
                pltpu.VMEM(outputs.shape, low),
                pltpu.VMEM((devices, 16, HEAD_DIM), low),
                pltpu.VMEM((devices, 16, HEAD_DIM), low),
                pltpu.VMEM((2 * BLOCK, HEAD_DIM), low),
                pltpu.VMEM((2, 2 * BLOCK, width), low),
                pltpu.VMEM((band, HEAD_DIM), low),
                pltpu.VMEM((band, 2 * HEAD_DIM), low),
                pltpu.VMEM((HEAD_DIM, band), low),
                pltpu.VMEM((2, band, HEAD_DIM), full),
                pltpu.VMEM((2 * BLOCK, width), low),
                pltpu.VMEM((band // rows, 2, rows, HEAD_DIM), low),
                pltpu.VMEM((devices // 2, 2, rows, HEAD_DIM), low),
                pltpu.VMEM((2, devices, 2, rows, HEAD_DIM), low),
                dma((3,)),
                dma((2,)),
                dma((2,)),
                dma((2,)),
                dma,
                dma((3,)),
                dma,
                dma((2,)),
                dma,
                dma((9,)),
            ],
            compiler_params=pltpu.CompilerParams(
                collective_id=0,
                has_side_effects=True,
                vmem_limit_bytes=63 * 1024 * 1024,
            ),
            cost_estimate=pl.CostEstimate(
                flops=48 * 5 * 2 * 256 * 256 * 128, bytes_accessed=8_000_000, transcendentals=0
            ),
        )(queries, keys, values, outputs, grad_out, first_block)
        return pl.pallas_call(
            functools.partial(finish, pieces),
            out_shape=(
                jax.ShapeDtypeStruct(queries.shape, low),
                jax.ShapeDtypeStruct(keys.shape, low),
                jax.ShapeDtypeStruct(values.shape, low),
            ),
            in_specs=[hbm] * 2,
            out_specs=(hbm,) * 3,
            scratch_shapes=[
                pltpu.VMEM(queries.shape, low),
                pltpu.VMEM((2, *keys.shape), low),
                dma((pieces + 2,)),
                dma((pieces + 2,)),
            ],
            compiler_params=pltpu.CompilerParams(vmem_limit_bytes=63 * 1024 * 1024),
        )(dq, dkv)

    placed = P(("ctx", "head"), None)
    return jax.shard_map(
        local,
        mesh=mesh,
        in_specs=(placed,) * 5 + (P(),),
        out_specs=(placed,) * 3,
        check_vma=False,
    )
```

```python
import functools
import math

import jax
import jax.numpy as jnp
from jax import lax
from jax.experimental import pallas as pl
from jax.experimental.pallas import tpu as pltpu
from jax.sharding import PartitionSpec as P

HEAD_DIM = 128
BLOCK = 256
WINDOW = 4
MESH = pl.DeviceIdType.MESH
FAR = 1e30


def contract_last(a, b):
    return lax.dot_general(a, b, (((1,), (1,)), ((), ())), preferred_element_type=jnp.float32)


def kernel(
    parts,
    devices,
    group,
    q_hbm,
    k_hbm,
    v_hbm,
    o_hbm,
    g_hbm,
    first_ref,
    dq_hbm,
    dkv_ref,
    q_own,
    g_own,
    o_own,
    corr_out,
    corr_in,
    corr_cols,
    qg,
    k_band,
    v_band,
    k_turned,
    scores_a,
    scores_b,
    grads_a,
    grads_b,
    total,
    dq_out,
    terms,
    far_terms,
    arrived,
    load_sem,
    kv_sem,
    near_sem,
    far_sem,
    corr_sem,
    qg_sem,
    dq_sem,
    term_sem,
    far_term_sem,
    send_sem,
):
    rows = 2 * BLOCK // devices
    half = devices // 2
    width = group * HEAD_DIM
    span = 2 * BLOCK
    own = 3 * BLOCK
    scaling = HEAD_DIM ** (-0.5)
    to_exp2 = scaling * math.log2(math.e)
    p = lax.axis_index("ctx")
    h = lax.axis_index("head")

    def at(shift):
        return lax.rem(p + shift + parts, parts)

    def other(off):
        return lax.rem(h + off, devices)

    barrier = pltpu.get_barrier_semaphore()

    def greet_row(off, carry):
        pl.semaphore_signal(barrier, inc=1, device_id=(p, other(off)), device_id_type=MESH)
        return carry

    lax.fori_loop(1, devices, greet_row, 0)
    has_earlier, has_later = p >= 1, p <= parts - 2
    has_second_earlier = p >= 2
    for shift, exists in ((1, has_later), (-1, has_earlier)):

        @pl.when(exists)
        def _():
            def greet_near(off, carry):
                pl.semaphore_signal(
                    barrier, inc=1, device_id=(at(shift), other(off)), device_id_type=MESH
                )
                return carry

            lax.fori_loop(0, devices, greet_near, 0)

    load_q = pltpu.make_async_copy(q_hbm, q_own, load_sem.at[0])
    load_g = pltpu.make_async_copy(g_hbm, g_own, load_sem.at[1])
    load_o = pltpu.make_async_copy(o_hbm, o_own, load_sem.at[2])
    load_q.start()
    load_g.start()
    load_o.start()

    @pl.when(p == 0)
    def _():
        k_band[BLOCK:own] = jnp.zeros((2 * BLOCK, HEAD_DIM), jnp.bfloat16)
        v_band[BLOCK:own, 0:HEAD_DIM] = jnp.zeros((2 * BLOCK, HEAD_DIM), jnp.bfloat16)

    @pl.when(p <= 1)
    def _():
        k_band[0:BLOCK] = jnp.zeros((BLOCK, HEAD_DIM), jnp.bfloat16)
        v_band[0:BLOCK, 0:HEAD_DIM] = jnp.zeros((BLOCK, HEAD_DIM), jnp.bfloat16)

    @pl.when(p == parts - 1)
    def _():
        arrived[1] = jnp.zeros((devices, 2, rows, HEAD_DIM), jnp.bfloat16)

    @pl.when((p == 0) | (p == parts - 1))
    def _():
        far_terms[...] = jnp.zeros((half, 2, rows, HEAD_DIM), jnp.bfloat16)

    after = parts - 1 - p
    neighbours = (p + parts - 1) // parts + (after + parts - 1) // parts
    pl.semaphore_wait(barrier, devices - 1 + devices * neighbours)

    def rows_at(start, count):
        return pl.ds(pl.multiple_of(start, 64), count)

    def lanes_at(start, count):
        return pl.ds(pl.multiple_of(start, HEAD_DIM), count)

    mine = rows_at(h * rows, rows)
    mine_kv = rows_at(own + h * rows, rows)

    for index, source, band in ((0, k_hbm, k_band), (1, v_hbm, v_band)):

        def send_kv(off, carry):
            d = other(off)
            pltpu.make_async_remote_copy(
                src_ref=source.at[:, lanes_at(d * HEAD_DIM, HEAD_DIM)],
                dst_ref=band.at[mine_kv, 0:HEAD_DIM],
                send_sem=send_sem.at[0],
                recv_sem=kv_sem.at[index],
                device_id=(p, d),
                device_id_type=MESH,
            ).start()
            return carry

        lax.fori_loop(1, devices, send_kv, 0)
        pltpu.make_async_copy(
            source.at[:, lanes_at(h * HEAD_DIM, HEAD_DIM)], band.at[mine_kv, 0:HEAD_DIM], kv_sem.at[index]
        ).start()

    def send_heads(i, count, sem):
        for index, source in ((0, q_own), (1, g_own)):

            def send_part(off, carry):
                d = other(off)
                pltpu.make_async_remote_copy(
                    src_ref=source.at[:, lanes_at(d * width + i * HEAD_DIM, count * HEAD_DIM)],
                    dst_ref=qg.at[index, mine, lanes_at(i * HEAD_DIM, count * HEAD_DIM)],
                    send_sem=send_sem.at[2],
                    recv_sem=qg_sem.at[sem],
                    device_id=(p, d),
                    device_id_type=MESH,
                ).start()
                return carry

            lax.fori_loop(1, devices, send_part, 0)
            pltpu.make_async_copy(
                source.at[:, lanes_at(h * width + i * HEAD_DIM, count * HEAD_DIM)],
                qg.at[index, mine, lanes_at(i * HEAD_DIM, count * HEAD_DIM)],
                qg_sem.at[sem],
            ).start()

    def wait_heads(i, count, sem):
        part = qg.at[:, :, i * HEAD_DIM : (i + count) * HEAD_DIM]
        pltpu.make_async_copy(part, part, qg_sem.at[sem]).wait()

    load_q.wait()
    load_g.wait()
    send_heads(0, 2, 0)


    load_o.wait()
    row_of = lax.broadcasted_iota(jnp.int32, (16, width), 0)
    col_of = lax.broadcasted_iota(jnp.int32, (16, width), 1)
    pick = jnp.where((row_of % 8) == col_of // HEAD_DIM, 1.0, 0.0).astype(jnp.bfloat16)
    upper = lax.broadcasted_iota(jnp.int32, (16, rows), 0) < 8
    corr_out[...] = jnp.zeros_like(corr_out)
    for d in range(devices):
        cols = slice(d * width, (d + 1) * width)
        product = g_own[:, cols].astype(jnp.float32) * o_own[:, cols].astype(jnp.float32)
        high = product.astype(jnp.bfloat16)
        low = (product - high.astype(jnp.float32)).astype(jnp.bfloat16)
        corr = contract_last(pick, high) + contract_last(pick, low)
        corr_high = corr.astype(jnp.bfloat16).astype(jnp.float32)
        corr_out[d, :, 0:rows] = jnp.where(upper, corr_high, corr - corr_high).astype(jnp.bfloat16)

    def send_corr(off, carry):
        d = other(off)
        pltpu.make_async_remote_copy(
            src_ref=corr_out.at[d],
            dst_ref=corr_in.at[h],
            send_sem=send_sem.at[1],
            recv_sem=corr_sem,
            device_id=(p, d),
            device_id_type=MESH,
        ).start()
        return carry

    lax.fori_loop(1, devices, send_corr, 0)
    pltpu.make_async_copy(corr_out.at[h], corr_in.at[h], corr_sem).start()
    total[...] = jnp.zeros_like(total)
    v_band[:, HEAD_DIM:] = jnp.full((5 * BLOCK, HEAD_DIM), -1.0, jnp.bfloat16)


    near, far = [], []
    for index, band in ((0, k_band), (1, v_band)):
        held = band.at[own : own + span, 0:HEAD_DIM]
        pltpu.make_async_copy(held, held, kv_sem.at[index]).wait()
        near.append(
            pltpu.make_async_remote_copy(
                src_ref=held,
                dst_ref=band.at[BLOCK : BLOCK + span, 0:HEAD_DIM],
                send_sem=send_sem.at[3],
                recv_sem=near_sem.at[index],
                device_id=(at(1), h),
                device_id_type=MESH,
            )
        )
        pl.when(has_later)(near[index].start)
        far.append(
            pltpu.make_async_remote_copy(
                src_ref=band.at[2 * BLOCK : 3 * BLOCK, 0:HEAD_DIM],
                dst_ref=band.at[0:BLOCK, 0:HEAD_DIM],
                send_sem=send_sem.at[4],
                recv_sem=far_sem.at[index],
                device_id=(at(1), h),
                device_id_type=MESH,
            )
        )
    send_heads(2, 2, 1)

    def turn(block):
        part = slice(block * BLOCK, (block + 1) * BLOCK)
        k_turned[:, part] = k_band[part].astype(jnp.float32).T.astype(jnp.bfloat16)

    turn(3)
    turn(4)
    pl.when(has_earlier)(near[0].wait_recv)
    pl.when(has_earlier & has_later)(far[0].start)
    turn(1)
    turn(2)

    pltpu.make_async_copy(corr_in, corr_in, corr_sem).wait()
    for d in range(devices):
        piece = corr_in[d].astype(jnp.float32)
        square = jnp.concatenate([piece, jnp.zeros((112, HEAD_DIM), jnp.float32)], axis=0).T
        corr_cols[d * rows : (d + 1) * rows] = square[0:rows].astype(jnp.bfloat16)

    pl.when(has_earlier)(near[1].wait_recv)
    pl.when(has_earlier & has_later)(far[1].start)
    send_heads(4, 2, 2)


    def round_terms(start, count):
        for r in range(start, start + count):
            part = slice(r * rows, (r + 1) * rows)
            terms[r, 0] = (total[0, part] * scaling).astype(jnp.bfloat16)
            terms[r, 1] = total[1, part].astype(jnp.bfloat16)

    def term_copy(r, distance, d):
        return pltpu.make_async_remote_copy(
            src_ref=terms.at[r],
            dst_ref=arrived.at[distance, h],
            send_sem=send_sem.at[6 + 2 * distance],
            recv_sem=term_sem.at[distance],
            device_id=(at(-distance), d),
            device_id_type=MESH,
        )

    pass_back = pltpu.make_async_remote_copy(
        src_ref=terms.at[0:half],
        dst_ref=far_terms,
        send_sem=send_sem.at[7],
        recv_sem=far_term_sem,
        device_id=(at(-1), h),
        device_id_type=MESH,
    )

    def send_dq(i, count):
        cols = slice(i * HEAD_DIM, (i + count) * HEAD_DIM)
        target = dq_hbm.at[:, lanes_at(h * width + i * HEAD_DIM, count * HEAD_DIM)]

        def send_part(off, carry):
            d = other(off)
            pltpu.make_async_remote_copy(
                src_ref=dq_out.at[rows_at(d * rows, rows), cols],
                dst_ref=target,
                send_sem=send_sem.at[5],
                recv_sem=dq_sem,
                device_id=(p, d),
                device_id_type=MESH,
            ).start()
            return carry

        lax.fori_loop(1, devices, send_part, 0)
        pltpu.make_async_copy(dq_out.at[mine, cols], target, dq_sem).start()

    def send_half(i, count, late):
        cols = slice(i * HEAD_DIM, (i + count) * HEAD_DIM)
        target = dq_hbm.at[:, lanes_at(h * width + i * HEAD_DIM, count * HEAD_DIM)]

        def send_part(d, carry):
            source = dq_out.at[rows_at(d * rows, rows), cols]

            @pl.when(d != h)
            def _():
                pltpu.make_async_remote_copy(
                    src_ref=source,
                    dst_ref=target,
                    send_sem=send_sem.at[5],
                    recv_sem=dq_sem,
                    device_id=(p, d),
                    device_id_type=MESH,
                ).start()

            @pl.when(d == h)
            def _():
                pltpu.make_async_copy(source, target, dq_sem).start()

            return carry

        lax.fori_loop(late * half, (late + 1) * half, send_part, 0)

    reach = WINDOW * BLOCK
    held_scores, held_grads = (scores_a, scores_b), (grads_a, grads_b)
    lane = lax.broadcasted_iota(jnp.int32, (BLOCK, HEAD_DIM), 1)

    def operands(late, i):
        query_rows = rows_at(late * BLOCK, BLOCK)
        key_rows = rows_at(late * BLOCK, reach)
        heads = [lanes_at((i + n) * HEAD_DIM, HEAD_DIM) for n in range(2)]
        return query_rows, key_rows, heads

    def products(slot, late, i):
        query_rows, key_rows, heads = operands(late, i)
        q = jnp.concatenate([qg[0, query_rows, cols] for cols in heads], axis=0)
        g = jnp.concatenate([qg[1, query_rows, cols] for cols in heads], axis=0)
        corr = corr_cols[query_rows, :].astype(jnp.float32)
        corr = jnp.concatenate(
            [
                jnp.where((lane == i + n) | (lane == i + n + 8), corr, 0.0).astype(jnp.bfloat16)
                for n in range(2)
            ],
            axis=0,
        )
        held_scores[slot][...] = contract_last(k_band[key_rows, :], q)
        held_grads[slot][...] = contract_last(
            v_band[key_rows, :], jnp.concatenate([g, corr], axis=1)
        )

    def returns(slot, late, i):
        query_rows, key_rows, heads = operands(late, i)
        q = jnp.concatenate([qg[0, query_rows, cols] for cols in heads], axis=0)
        g = jnp.concatenate([qg[1, query_rows, cols] for cols in heads], axis=0)
        score = held_scores[slot][...]
        grads = held_grads[slot][...]
        first = first_ref[2 * p + late]
        tiles = [score[t * BLOCK : (t + 1) * BLOCK] for t in range(WINDOW)]
        biases = [
            jnp.where(first <= 2 * p + late - 3 + t, 0.0, -FAR).astype(jnp.float32)
            for t in range(WINDOW)
        ]
        peak = None
        for t in range(WINDOW):
            top = jnp.max(tiles[t], axis=0, keepdims=True) + biases[t]
            peak = top if peak is None else jnp.maximum(peak, top)
        level = peak * to_exp2
        weights = [
            jnp.exp2(tiles[t] * to_exp2 - (level - biases[t])) for t in range(WINDOW)
        ]
        weights = jnp.concatenate(weights, axis=0)
        probs = weights * (1.0 / jnp.sum(weights, axis=0, keepdims=True))
        grad_scores = (probs * grads).astype(jnp.bfloat16)
        total[0, key_rows, :] += jnp.dot(grad_scores, q, preferred_element_type=jnp.float32)
        total[1, key_rows, :] += jnp.dot(
            probs.astype(jnp.bfloat16), g, preferred_element_type=jnp.float32
        )
        dq_turned = jnp.dot(
            k_turned[:, lanes_at(late * BLOCK, reach)],
            grad_scores,
            preferred_element_type=jnp.float32,
        )
        dq = (dq_turned * scaling).T.astype(jnp.bfloat16)
        for n in range(2):
            dq_out[query_rows, heads[n]] = dq[n * BLOCK : (n + 1) * BLOCK]

    wait_heads(0, 2, 0)
    products(0, 1, 0)
    returns(0, 1, 0)
    pl.when(has_second_earlier)(far[0].wait_recv)
    pl.when(has_second_earlier)(far[1].wait_recv)
    turn(0)
    products(1, 0, 0)
    wait_heads(2, 2, 1)
    products(0, 1, 2)
    returns(1, 0, 0)
    products(1, 0, 2)
    send_dq(0, 2)
    returns(0, 1, 2)
    returns(1, 0, 2)
    send_dq(2, 2)
    wait_heads(4, 2, 2)
    products(0, 0, 4)
    products(1, 1, 4)
    returns(0, 0, 4)
    round_terms(0, half)
    pl.when(has_second_earlier)(pass_back.start)
    send_half(4, 2, 0)
    returns(1, 1, 4)

    def send_near(d, carry):
        term_copy(half + d, 1, d).start()
        return carry

    def send_own(off, carry):
        d = other(off)
        term_copy(half + devices + d, 0, d).start()
        return carry

    round_terms(half, half)

    @pl.when(has_earlier)
    def _():
        lax.fori_loop(0, half, send_near, 0)

    round_terms(half + devices, devices)
    lax.fori_loop(1, devices, send_own, 0)
    pltpu.make_async_copy(
        terms.at[half + devices + h], arrived.at[0, h], term_sem.at[0]
    ).start()
    send_half(4, 2, 1)

    pl.when(has_earlier & has_later)(pass_back.wait_recv)
    for r in range(half):
        at_row = devices + r
        part = slice(at_row * rows, (at_row + 1) * rows)
        terms[at_row, 0] = (
            total[0, part] * scaling + far_terms[r, 0].astype(jnp.float32)
        ).astype(jnp.bfloat16)
        terms[at_row, 1] = (total[1, part] + far_terms[r, 1].astype(jnp.float32)).astype(
            jnp.bfloat16
        )

    @pl.when(has_earlier)
    def _():
        lax.fori_loop(half, devices, send_near, 0)

    pltpu.make_async_copy(arrived.at[0], arrived.at[0], term_sem.at[0]).wait()
    pl.when(has_later)(
        pltpu.make_async_copy(arrived.at[1], arrived.at[1], term_sem.at[1]).wait
    )
    for d in range(devices):
        cols = slice(d * HEAD_DIM, (d + 1) * HEAD_DIM)
        for index in range(2):
            held = arrived[0, d, index].astype(jnp.float32)
            more = arrived[1, d, index].astype(jnp.float32)
            dkv_ref[index, :, cols] = (held + more).astype(jnp.bfloat16)
    pltpu.make_async_copy(dq_hbm, dq_hbm, dq_sem).wait()

    most = span - rows

    def left(view, index):
        pltpu.make_async_copy(view, view, send_sem.at[index]).wait()

    left(k_band.at[0 : 2 * most], 0)
    left(corr_in.at[0 : devices - 1], 1)
    left(qg.at[:, 0:most], 2)
    left(dq_out.at[0:most], 5)
    left(terms.at[0 : devices - 1], 6)

    @pl.when(has_later)
    def _():
        left(k_band.at[0 : 2 * span], 3)

    @pl.when(has_earlier & has_later)
    def _():
        left(k_band.at[0 : 2 * BLOCK], 4)

    @pl.when(has_earlier)
    def _():
        left(terms.at[0:devices], 8)

    pl.when(has_second_earlier)(pass_back.wait_send)


def finish(pieces, dq, dkv, dq_hbm, dk_hbm, dv_hbm, held, held_kv, in_sem, out_sem):
    rows = held.shape[0] // pieces
    legs = []
    for n in range(pieces):
        part = slice(n * rows, (n + 1) * rows)
        legs.append((dq.at[part], held.at[part], dq_hbm.at[part]))
    legs.append((dkv.at[0], held_kv.at[0], dk_hbm))
    legs.append((dkv.at[1], held_kv.at[1], dv_hbm))
    loads, stores = [], []
    for n, (source, between, target) in enumerate(legs):
        loads.append(pltpu.make_async_copy(source, between, in_sem.at[n]))
        stores.append(pltpu.make_async_copy(between, target, out_sem.at[n]))
        loads[n].start()
    for n in range(len(legs)):
        loads[n].wait()
        stores[n].start()
    for n in range(len(legs)):
        stores[n].wait()


def solution(mesh):
    parts = mesh.shape["ctx"]
    devices = mesh.shape["head"]
    rows = 2 * BLOCK // devices

    def local(queries, keys, values, outputs, grad_out, first_block):
        group = queries.shape[1] // keys.shape[1]
        hbm = pl.BlockSpec(memory_space=pl.ANY)
        vmem = pl.BlockSpec(memory_space=pltpu.VMEM)
        low, full = jnp.bfloat16, jnp.float32
        dma = pltpu.SemaphoreType.DMA
        width = queries.shape[1] // devices
        pieces = 4
        band = 5 * BLOCK
        dq, dkv = pl.pallas_call(
            functools.partial(kernel, parts, devices, group),
            out_shape=(
                jax.ShapeDtypeStruct(queries.shape, low),
                jax.ShapeDtypeStruct((2, *keys.shape), low),
            ),
            in_specs=[hbm] * 5 + [pl.BlockSpec(memory_space=pltpu.SMEM)],
            out_specs=(hbm, vmem),
            scratch_shapes=[
                pltpu.VMEM(queries.shape, low),
                pltpu.VMEM(grad_out.shape, low),
                pltpu.VMEM(outputs.shape, low),
                pltpu.VMEM((devices, 16, HEAD_DIM), low),
                pltpu.VMEM((devices, 16, HEAD_DIM), low),
                pltpu.VMEM((2 * BLOCK, HEAD_DIM), low),
                pltpu.VMEM((2, 2 * BLOCK, width), low),
                pltpu.VMEM((band, HEAD_DIM), low),
                pltpu.VMEM((band, 2 * HEAD_DIM), low),
                pltpu.VMEM((HEAD_DIM, band), low),
                pltpu.VMEM((WINDOW * BLOCK, 2 * BLOCK), full),
                pltpu.VMEM((WINDOW * BLOCK, 2 * BLOCK), full),
                pltpu.VMEM((WINDOW * BLOCK, 2 * BLOCK), full),
                pltpu.VMEM((WINDOW * BLOCK, 2 * BLOCK), full),
                pltpu.VMEM((2, band, HEAD_DIM), full),
                pltpu.VMEM((2 * BLOCK, width), low),
                pltpu.VMEM((band // rows, 2, rows, HEAD_DIM), low),
                pltpu.VMEM((devices // 2, 2, rows, HEAD_DIM), low),
                pltpu.VMEM((2, devices, 2, rows, HEAD_DIM), low),
                dma((3,)),
                dma((2,)),
                dma((2,)),
                dma((2,)),
                dma,
                dma((3,)),
                dma,
                dma((2,)),
                dma,
                dma((9,)),
            ],
            compiler_params=pltpu.CompilerParams(
                collective_id=0,
                has_side_effects=True,
                vmem_limit_bytes=63 * 1024 * 1024,
            ),
            cost_estimate=pl.CostEstimate(
                flops=48 * 5 * 2 * 256 * 256 * 128, bytes_accessed=8_000_000, transcendentals=0
            ),
        )(queries, keys, values, outputs, grad_out, first_block)
        return pl.pallas_call(
            functools.partial(finish, pieces),
            out_shape=(
                jax.ShapeDtypeStruct(queries.shape, low),
                jax.ShapeDtypeStruct(keys.shape, low),
                jax.ShapeDtypeStruct(values.shape, low),
            ),
            in_specs=[hbm] * 2,
            out_specs=(hbm,) * 3,
            scratch_shapes=[
                pltpu.VMEM(queries.shape, low),
                pltpu.VMEM((2, *keys.shape), low),
                dma((pieces + 2,)),
                dma((pieces + 2,)),
            ],
            compiler_params=pltpu.CompilerParams(vmem_limit_bytes=63 * 1024 * 1024),
        )(dq, dkv)

    placed = P(("ctx", "head"), None)
    return jax.shard_map(
        local,
        mesh=mesh,
        in_specs=(placed,) * 5 + (P(),),
        out_specs=(placed,) * 3,
        check_vma=False,
    )
```
